128 devices in a mesh: grp: 16 (over z, x_hi, core), sp: 8 (over y, x_lo).
Axes of the slice: x: 4 (x_hi: 2, x_lo: 2; x = x_hi * 2 + x_lo), y: 4, z: 4, core: 2. Of those that a mesh axis runs over, the one named last changes fastest.
Arguments:
- image_tokens: bfloat16 [32, 8, 64, 3072], P('grp', 'sp'), may hold values from -6 to 6
- text_tokens: bfloat16 [256, 3072], replicated, may hold values from -6 to 6
- mod_shift: float32 [3072], replicated, may hold values from -3 to 3
- mod_scale: float32 [3072], replicated, may hold values from -0.5 to 0.5
- mod_gate: float32 [3072], replicated, may hold values from 0.5 to 1.5
- w_qkv: bfloat16 [3072, 3, 2048], P(None, None, 'sp'), may hold values from -0.109375 to 0.109375
- w_text_kv: bfloat16 [3072, 2, 2048], P(None, None, 'sp'), may hold values from -0.109375 to 0.109375
- q_gain: float32 [128], replicated, may hold values from 1.5 to 2.5
- k_gain: float32 [128], replicated, may hold values from 1.5 to 2.5
- text_gain: float32 [128], replicated, may hold values from 1.5 to 2.5
- w_out: bfloat16 [2048, 3072], P('sp'), may hold values from -0.125 to 0.125
- w_final: bfloat16 [3072, 64], replicated, may hold values from -0.109375 to 0.109375
- w_conv_in: bfloat16 [3, 3, 3, 16, 256], replicated, may hold values from -0.3125 to 0.3125
- w_conv_mid: bfloat16 [3, 3, 3, 256, 256], replicated, may hold values from -0.078125 to 0.078125
- clip_ids: int32 [32], replicated, may hold values from 0 to 7, never falling along the last dimension, each value on 1 to 8 neighbouring positions
Outputs:
- block_out: bfloat16 [32, 8, 64, 3072], P('grp', 'sp')
- decoded: bfloat16 [32, 16, 128, 256], P('grp', 'sp')
The draws below stay inside these ranges and needn't reach their ends.
Inputs may be any that keep to these rules, and one draw needn't show every extreme that they name: `clip_ids`: clip numbers never fall along the frames, every number from 0 to 7 appears, and each clip spans 1 to 8 consecutive frames.
All inputs are finite; a program needn't handle non-finite values.
Results may differ from the reference program's by a relative error of at most 0.02.
Values may be sent and summed in bfloat16 or wider, within the bound.
A program may use at most 128 MiB of HBM per device.

```python
import math
import jax
import jax.numpy as jnp
import numpy as np
from jax import lax

D = 3072
LAT = 16
HEADS = 16
HD = 128
TXT = 256
CV = 256
WP = 64
FRAMES = 32
HP = 8


def shard_levels(stream_key, extent, split, least, high):
    loudness = 1.0
    for axis_at, shards_of in split:
        steps = jax.random.uniform(jax.random.fold_in(jax.random.fold_in(stream_key, 6), axis_at), (shards_of,), jnp.float32, least / len(split), high / len(split))
        loudness = loudness * jnp.repeat(jnp.exp(steps), extent[axis_at] // shards_of).reshape((-1,) + (1,) * (len(extent) - 1 - axis_at))
    return loudness


def profile(count, total, bound, slope):
    portions = [(1 << 20) // math.isqrt(rank ** slope) + 1 for rank in range(2, count + 1)]
    surplus, counts = total - bound - (count - 1), [1] * (count - 1)
    while surplus > 0:
        movable = [i for i in range(count - 1) if counts[i] < bound]
        pool, budget = sum([portions[i] for i in movable]), surplus
        for i in movable:
            extra = min(bound - counts[i], max(1, budget * portions[i] // pool), surplus)
            counts[i] = counts[i] + extra
            surplus = surplus - extra
    return np.array([bound] + counts)


def uneven_parts(rng, number_of, total, bound, slope):
    if number_of == 2:
        one = jax.random.randint(rng, (), max(1, total - bound), min(bound, total - 1) + 1)
        return jnp.stack([one, total - one])
    lengths = jnp.asarray(profile(number_of, total, bound, slope), jnp.int32)
    pairs = (number_of - 1) // 2
    donor, receiver = lengths[1:1 + 2 * pairs:2], lengths[2:2 + 2 * pairs:2]
    margin = jnp.minimum(donor - 1, bound - receiver)
    shifted = jax.random.randint(jax.random.fold_in(rng, 1), (pairs,), 0, 1 << 20) % (margin + 1)
    lengths = lengths.at[1:1 + 2 * pairs:2].set(donor - shifted).at[2:2 + 2 * pairs:2].set(receiver + shifted)
    return lengths[jax.random.permutation(jax.random.fold_in(rng, 2), number_of)]


def normal_values(rng, shape, scale, bound, pieces=(), kind=jnp.bfloat16):
    array = jax.random.normal(rng, shape, jnp.float32) * scale
    if len(pieces) > 0:
        array = shard_levels(rng, shape, pieces, -0.22, 0.18) * array
    return jnp.clip(array, min=-bound, max=bound).astype(kind)


def setup_inputs(seed: int = 0) -> dict:
    key_of = jax.random.split(jax.random.key(seed), 16)
    return {
        "image_tokens": normal_values(key_of[0], (FRAMES, HP, WP, D), 1.0, 6.0, ((0, 16), (1, 8))),
        "text_tokens": normal_values(key_of[1], (TXT, D), 1.0, 6.0),
        "mod_shift": normal_values(key_of[2], (D,), 0.5, 3.0, (), jnp.float32),
        "mod_scale": jnp.clip(jax.random.uniform(key_of[3], (D,), jnp.float32, -0.5, 0.5), -0.5, 0.5),
        "mod_gate": jnp.clip(jax.random.uniform(key_of[4], (D,), jnp.float32, 0.5, 1.5), 0.5, 1.5),
        "w_qkv": normal_values(key_of[5], (D, 3, HEADS * HD), D ** -0.5, 0.109375, ((2, 8),)),
        "w_text_kv": normal_values(key_of[6], (D, 2, HEADS * HD), D ** -0.5, 0.109375, ((2, 8),)),
        "q_gain": jnp.clip(jnp.exp(jax.random.uniform(key_of[7], (HD,), jnp.float32, math.log(1.5), math.log(2.5))), 1.5, 2.5),
        "k_gain": jnp.clip(jnp.exp(jax.random.uniform(key_of[8], (HD,), jnp.float32, math.log(1.5), math.log(2.5))), 1.5, 2.5),
        "text_gain": jnp.clip(jnp.exp(jax.random.uniform(key_of[9], (HD,), jnp.float32, math.log(1.5), math.log(2.5))), 1.5, 2.5),
        "w_out": normal_values(key_of[10], (HEADS * HD, D), (HEADS * HD) ** -0.5, 0.125, ((0, 8),)),
        "w_final": normal_values(key_of[11], (D, 4 * LAT), D ** -0.5, 0.109375),
        "w_conv_in": normal_values(key_of[12], (3, 3, 3, LAT, CV), (27 * LAT) ** -0.5, 0.3125),
        "w_conv_mid": normal_values(key_of[13], (3, 3, 3, CV, CV), (27 * CV) ** -0.5, 0.078125),
        "clip_ids": jnp.searchsorted(jnp.cumsum(uneven_parts(key_of[14], FRAMES // 4, FRAMES, 8, 1)), jnp.arange(FRAMES), side="right").astype(jnp.int32),
    }


EPS = 1e-06

def layer_norm(values):
    middle = lax.optimization_barrier(jnp.mean(values, axis=-1, keepdims=True))
    centered = values - middle
    spread = lax.optimization_barrier(jnp.mean(centered * centered, axis=-1, keepdims=True))
    return centered * lax.rsqrt(spread + EPS)

def rms_scale(values, gain):
    return values * lax.rsqrt(lax.optimization_barrier(jnp.mean(values * values, axis=-1, keepdims=True)) + EPS) * gain

def causal_conv(field, weight, starts):
    frames = field.shape[0]
    height = field.shape[1]
    breadth = field.shape[2]
    depth = weight.shape[3]
    width_out = weight.shape[4]
    padded = jnp.pad(field, ((0, 0), (1, 1), (1, 1), (0, 0)))
    order = jnp.arange(frames, dtype=jnp.int32)
    total = jnp.zeros((frames * height * breadth, width_out), jnp.float32)
    for shift_t in range(3):
        index = jnp.maximum(order - shift_t, starts).astype(jnp.int32)
        taken = jnp.take(padded, index, axis=0)
        for shift_r in range(3):
            for shift_c in range(3):
                patch_view = taken[:, shift_r:shift_r + height, shift_c:shift_c + breadth, :]
                total = total + jnp.dot(patch_view.reshape(-1, depth).astype(jnp.float32), weight[shift_t, shift_r, shift_c].astype(jnp.float32))
    return total.reshape(frames, height, breadth, width_out)

def reference(image_tokens, text_tokens, mod_shift, mod_scale, mod_gate, w_qkv, w_text_kv, q_gain, k_gain, text_gain, w_out, w_final, w_conv_in, w_conv_mid, clip_ids):
    count = FRAMES * HP * WP
    inner = HEADS * HD
    tokens = image_tokens.reshape(count, D)
    residual_in = tokens.astype(jnp.float32)
    normed = (layer_norm(residual_in) * (1.0 + mod_scale) + mod_shift).astype(jnp.bfloat16)
    projected = jnp.dot(normed.astype(jnp.float32), w_qkv.reshape(D, 3 * inner).astype(jnp.float32)).reshape(count, 3, HEADS, HD)
    queries = rms_scale(projected[:, 0], q_gain).astype(jnp.bfloat16)
    keys = rms_scale(projected[:, 1], k_gain).astype(jnp.bfloat16)
    values = projected[:, 2].astype(jnp.bfloat16)
    text_normed = layer_norm(text_tokens.astype(jnp.float32)).astype(jnp.bfloat16)
    text_projected = jnp.dot(text_normed.astype(jnp.float32), w_text_kv.reshape(D, 2 * inner).astype(jnp.float32)).reshape(TXT, 2, HEADS, HD)
    text_keys = rms_scale(text_projected[:, 0], text_gain).astype(jnp.bfloat16)
    text_values = text_projected[:, 1].astype(jnp.bfloat16)
    all_keys = jnp.concatenate([keys, text_keys], axis=0)
    all_values = jnp.concatenate([values, text_values], axis=0)
    q_heads = jnp.transpose(queries, (1, 0, 2)).astype(jnp.float32)
    k_heads = jnp.transpose(all_keys, (1, 0, 2)).astype(jnp.float32)
    v_heads = jnp.transpose(all_values, (1, 0, 2)).astype(jnp.float32)
    block = math.gcd(count, 1024)
    factor = HD ** (-0.5)

    def head_attention(operands):
        q_head, k_head, v_head = operands

        def query_block(q_block):
            scores = jnp.dot(q_block, k_head.T) * factor
            weights = lax.optimization_barrier(jnp.exp(scores).astype(jnp.bfloat16)).astype(jnp.float32)
            totals = lax.optimization_barrier(jnp.sum(weights, axis=1))
            weighted = jnp.dot(weights, v_head)
            return weighted / totals[:, None]
        return lax.map(query_block, q_head.reshape(count // block, block, HD)).reshape(count, HD)
    attended_heads = lax.map(head_attention, (q_heads, k_heads, v_heads))
    attended = jnp.transpose(attended_heads, (1, 0, 2)).reshape(count, inner).astype(jnp.bfloat16)
    proj = jnp.dot(attended.astype(jnp.float32), w_out.astype(jnp.float32))
    block_flat = (residual_in + mod_gate * proj).astype(jnp.bfloat16)
    final = layer_norm(block_flat.astype(jnp.float32)).astype(jnp.bfloat16)
    latent_flat = jnp.dot(final.astype(jnp.float32), w_final.astype(jnp.float32)).astype(jnp.bfloat16)
    latent = latent_flat.reshape(FRAMES, HP, WP, 2, 2, LAT).transpose(0, 1, 3, 2, 4, 5).reshape(FRAMES, 2 * HP, 2 * WP, LAT)
    starts = lax.optimization_barrier(jnp.sum((clip_ids[None, :] < clip_ids[:, None]).astype(jnp.int32), axis=1)).astype(jnp.int32)
    first_conv = causal_conv(latent, w_conv_in, starts)
    activated = jax.nn.silu(first_conv).astype(jnp.bfloat16)
    decoded = (causal_conv(activated, w_conv_mid, starts) + first_conv).astype(jnp.bfloat16)
    block_out = block_flat.reshape(FRAMES, HP, WP, D)
    return (block_out, decoded)
```

```python
import math

import jax
import jax.numpy as jnp
from jax import lax
from jax.experimental import pallas as pl
from jax.experimental.pallas import tpu as pltpu
from jax.sharding import PartitionSpec as P

HD = 128
EPS = 1e-06
MESH = pl.DeviceIdType.MESH
F32 = jnp.float32
BF16 = jnp.bfloat16


def layer_norm(values):
    middle = jnp.mean(values, axis=-1, keepdims=True)
    centered = values - middle
    spread = jnp.mean(centered * centered, axis=-1, keepdims=True)
    return centered * lax.rsqrt(spread + EPS)


def rms_scale(values, gain):
    return values * lax.rsqrt(jnp.mean(values * values, axis=-1, keepdims=True) + EPS) * gain


class Ring:
    def __init__(self, at, before, after, mate, piece, half, send, recv):
        self.at = at
        self.before, self.after, self.mate = before, after, mate
        self.piece, self.half = piece, half
        self.send, self.recv = send, recv

    def copy(self, i, slot, j, device):
        return pltpu.make_async_remote_copy(
            src_ref=slot,
            dst_ref=slot,
            send_sem=self.send.at[i, j],
            recv_sem=self.recv.at[i, j],
            device_id=device,
            device_id_type=MESH,
        )

    def place(self, step):
        return lax.rem(self.at + step, 4)

    def out(self, i, j):
        if j in (0, 1, 2):
            return self.copy(i, self.piece(i, self.at), j, (self.after, self.before, self.mate)[j])
        if j == 3:
            return self.copy(i, self.half(i, self.place(3), 0), j, self.after)
        if j == 5:
            return self.copy(i, self.half(i, self.place(1), 1), j, self.before)
        return self.copy(i, self.piece(i, self.place({4: 3, 6: 1, 7: 2}[j])), j, self.mate)

    def start(self, i, mate):
        for j in (0, 1, 2) if mate else (0, 1):
            self.out(i, j).start()

    def landed(self, i, j, mate_piece=None):
        slot = {
            0: lambda: self.piece(i, self.place(3)),
            1: lambda: self.piece(i, self.place(1)),
            3: lambda: self.half(i, self.place(2), 0),
            5: lambda: self.half(i, self.place(2), 1),
        }
        if j in slot:
            where = slot[j]()
        else:
            where = mate_piece(i, self.place({2: 0, 4: 3, 6: 1, 7: 2}[j]))
        self.copy(i, where, j, self.after).wait_recv()

    def forward(self, i, mate):
        self.landed(i, 0)
        self.out(i, 3).start()
        self.landed(i, 1)
        self.out(i, 5).start()
        if mate:
            self.out(i, 4).start()
            self.out(i, 6).start()

    def opposite(self, i, mate):
        self.landed(i, 3)
        self.landed(i, 5)
        if mate:
            self.out(i, 7).start()

    def finish(self, i, js):
        for j in js:
            self.out(i, j).wait_send()


def block_kernel(
    x_ref,
    shift_ref,
    scale_ref,
    gate_ref,
    w_qkv_ref,
    text_k_ref,
    text_v_ref,
    q_gain_ref,
    k_gain_ref,
    w_out_ref,
    w_final_ref,
    out_ref,
    lat_ref,
    tokens,
    weights,
    qkv,
    stage,
    stage_far,
    acc,
    totals,
    w_out,
    att_out,
    att,
    local_sem,
    copy_sem,
    wx_send,
    wx_recv,
    w_send,
    w_recv,
    t_send,
    t_recv,
    ox_send,
    ox_recv,
    o_send,
    o_recv,
    xa_send,
    xa_recv,
    xb_send,
    xb_recv,
    kv_send,
    kv_recv,
    at_send,
    at_recv,
):
    grp, sp = lax.axis_index("grp"), lax.axis_index("sp")
    z, xh, core = lax.div(grp, 4), lax.rem(lax.div(grp, 2), 2), lax.rem(grp, 2)
    y, xl = lax.div(sp, 2), lax.rem(sp, 2)
    x = 2 * xh + xl
    rows, width = x_ref.shape
    piece_rows = width // 8
    keys_here = 4 * rows
    out_half = width // 2

    def device(dz=0, dxh=0, dcore=0, dy=0, dxl=0):
        new_grp = 4 * lax.rem(z + dz, 4) + 2 * lax.rem(xh + dxh, 2) + lax.rem(core + dcore, 2)
        new_sp = 2 * lax.rem(y + dy, 4) + lax.rem(xl + dxl, 2)
        return (new_grp, new_sp)

    own_weights = pltpu.make_async_copy(w_qkv_ref, weights.at[xl], local_sem.at[0])
    own_weights.start()
    out_rows = pl.ds(pl.multiple_of(256 * sp, 256), 256)
    own_out = pltpu.make_async_copy(w_out_ref, w_out.at[out_rows], local_sem.at[1])
    own_out.start()

    plane = [(dx, dy) for dx in range(4) for dy in range(4) if dx or dy]

    def on_plane(dx, dy):
        to_x, to_y = lax.rem(x + dx, 4), lax.rem(y + dy, 4)
        return (4 * z + 2 * lax.div(to_x, 2) + core, 2 * to_y + lax.rem(to_x, 2))

    barrier = pltpu.get_barrier_semaphore()
    partners = [on_plane(dx, dy) for dx, dy in plane]
    partners += [device(dz=1), device(dz=3), device(dcore=1)]
    for partner in partners:
        pl.semaphore_signal(barrier, inc=1, device_id=partner, device_id_type=MESH)
    pl.semaphore_wait(barrier, len(partners))

    def weight_rows(place, c):
        return pl.ds(pl.multiple_of(piece_rows * (2 * place + c), 128), piece_rows)

    def weight_piece(i, place):
        return weights.at[1 - xl, (1, 2, 0)[i], weight_rows(place, core)]

    def weight_half(i, place, h):
        start = piece_rows * (2 * place + core) + h * (piece_rows // 2)
        return weights.at[1 - xl, (1, 2, 0)[i], pl.ds(pl.multiple_of(start, 64), piece_rows // 2)]

    def weight_mate(i, place):
        return weights.at[1 - xl, (1, 2, 0)[i], weight_rows(place, 1 - core)]

    def weight_hop(i):
        part = (1, 2, 0)[i]
        return pltpu.make_async_remote_copy(
            src_ref=w_qkv_ref.at[part, weight_rows(z, core)],
            dst_ref=weights.at[xl, part, weight_rows(z, core)],
            send_sem=wx_send.at[i],
            recv_sem=wx_recv.at[i],
            device_id=device(dxl=1),
            device_id_type=MESH,
        )

    w_ring = Ring(z, device(dz=3), device(dz=1), device(dcore=1), weight_piece, weight_half, w_send, w_recv)

    def weight_landed(i):
        slot = weight_piece(i, z)
        pltpu.make_async_remote_copy(
            src_ref=slot,
            dst_ref=slot,
            send_sem=wx_send.at[i],
            recv_sem=wx_recv.at[i],
            device_id=device(dxl=1),
            device_id_type=MESH,
        ).wait_recv()

    t_ring = Ring(
        y,
        device(dy=3),
        device(dy=1),
        None,
        lambda i, place: tokens.at[place],
        lambda i, place, h: tokens.at[place, pl.ds(h * (rows // 2), rows // 2)],
        t_send,
        t_recv,
    )

    for i in range(3):
        weight_hop(i).start()
    normed = layer_norm(x_ref[...].astype(F32)) * (1.0 + scale_ref[...]) + shift_ref[...]
    tokens[y] = normed.astype(BF16)
    t_ring.start(0, False)

    def out_piece_of(i, place, c):
        start = 256 * (2 * place + (xl if i == 0 else 1 - xl))
        return w_out.at[pl.ds(pl.multiple_of(start, 256), 256), pl.ds(pl.multiple_of(out_half * c, 128), out_half)]

    def out_half_of(i, place, h):
        start = 256 * (2 * place + (xl if i == 0 else 1 - xl)) + 128 * h
        return w_out.at[pl.ds(pl.multiple_of(start, 128), 128), pl.ds(pl.multiple_of(out_half * core, 128), out_half)]

    def out_piece(i, place):
        return out_piece_of(i, place, core)

    def out_mate(i, place):
        return out_piece_of(i, place, 1 - core)

    o_ring = Ring(y, device(dy=3), device(dy=1), device(dcore=1), out_piece, out_half_of, o_send, o_recv)

    def out_hop(slot):
        return pltpu.make_async_remote_copy(
            src_ref=slot,
            dst_ref=slot,
            send_sem=ox_send.at[0],
            recv_sem=ox_recv.at[0],
            device_id=device(dxl=1),
            device_id_type=MESH,
        )

    scale = HD ** (-0.5) / math.log(2.0)
    q_gain = q_gain_ref[...] * scale
    k_gain = k_gain_ref[...]
    block = 2 * z + core

    def finish_part(part, values):
        if part == 2:
            return values.astype(BF16)
        return rms_scale(values, q_gain if part == 0 else k_gain).astype(BF16)

    def near_copy(j, place, near):
        here = pl.ds(pl.multiple_of(place * rows, rows), rows)
        if near:
            return pltpu.make_async_copy(stage.at[j, xh], qkv.at[block, x, :, here], copy_sem.at[j])
        return pltpu.make_async_remote_copy(
            src_ref=stage.at[j, 1 - xh],
            dst_ref=qkv.at[block, x, :, here],
            send_sem=xa_send.at[j],
            recv_sem=xa_recv.at[j],
            device_id=device(dxh=1),
            device_id_type=MESH,
        )

    def near_heads(j, place):
        for part in (1, 2, 0):
            made = jnp.dot(tokens[place], weights[xl, part], preferred_element_type=F32)
            for head in range(2):
                stage[j, head, part] = finish_part(part, made[:, head * HD : (head + 1) * HD])
        for near in (False, True):
            near_copy(j, place, near).start()

    def far_copy(i, a):
        part = (1, 2, 0)[i]
        head = lax.rem(xh + a, 2)
        return pltpu.make_async_remote_copy(
            src_ref=stage_far.at[part, head],
            dst_ref=qkv.at[block, x, part],
            send_sem=xb_send.at[a, i],
            recv_sem=xb_recv.at[a, i],
            device_id=device(dxh=a, dxl=1),
            device_id_type=MESH,
        )

    def far_heads(i):
        part = (1, 2, 0)[i]
        all_tokens = tokens[...].reshape(4 * rows, width)
        made = jnp.dot(all_tokens, weights[1 - xl, part], preferred_element_type=F32)
        for head in range(2):
            stage_far[part, head] = finish_part(part, made[:, head * HD : (head + 1) * HD])
        for a in range(2):
            far_copy(i, a).start()

    places = [y, lax.rem(y + 3, 4), lax.rem(y + 1, 4), lax.rem(y + 2, 4)]
    weight_landed(0)
    w_ring.start(0, True)
    own_weights.wait()
    near_heads(0, places[0])
    weight_landed(1)
    w_ring.start(1, True)
    w_ring.forward(0, True)
    weight_landed(2)
    w_ring.start(2, True)
    own_out.wait()
    out_hop(out_piece(0, y)).start()
    w_ring.forward(1, True)
    t_ring.forward(0, False)
    w_ring.opposite(0, True)
    w_ring.forward(2, True)
    near_heads(1, places[1])
    near_heads(2, places[2])
    w_ring.opposite(1, True)
    w_ring.opposite(2, True)
    t_ring.opposite(0, False)
    o_ring.start(0, False)
    out_hop(out_piece(1, y)).wait_recv()
    o_ring.start(1, True)
    near_heads(3, places[3])
    for i in range(3):
        for j in (2, 4, 6, 7):
            w_ring.landed(i, j, weight_mate)
        far_heads(i)

    sources = [2 * lax.rem(xh + a, 2) + lax.rem(xl + b, 2) for b in range(2) for a in range(2)]

    def kv_piece_of(i, place, c):
        return qkv.at[2 * place + c, sources[i], pl.ds(1, 2)]

    def kv_piece(i, place):
        return kv_piece_of(i, place, core)

    def kv_half(i, place, h):
        return qkv.at[2 * place + core, sources[i], 1 + h]

    def kv_mate(i, place):
        return kv_piece_of(i, place, 1 - core)

    kv_ring = Ring(z, device(dz=3), device(dz=1), device(dcore=1), kv_piece, kv_half, kv_send, kv_recv)

    for j in range(4):
        near_copy(j, places[j], True).wait()
    kv_ring.start(0, True)
    for j in range(4):
        here = pl.ds(pl.multiple_of(places[j] * rows, rows), rows)
        slot = qkv.at[block, sources[1], :, here]
        pltpu.make_async_remote_copy(
            src_ref=slot,
            dst_ref=slot,
            send_sem=xa_send.at[j],
            recv_sem=xa_recv.at[j],
            device_id=device(dxh=1),
            device_id_type=MESH,
        ).wait_recv()
    kv_ring.start(1, True)
    for a in range(2):
        for i in range(3):
            slot = qkv.at[block, sources[2 + a], (1, 2, 0)[i]]
            pltpu.make_async_remote_copy(
                src_ref=slot,
                dst_ref=slot,
                send_sem=xb_send.at[a, i],
                recv_sem=xb_recv.at[a, i],
                device_id=device(dxl=1),
                device_id_type=MESH,
            ).wait_recv()
        kv_ring.start(2 + a, True)

    q_tile = 2 * keys_here

    def attend(first, keys, values, tile):
        here = pl.ds(tile * q_tile, q_tile)
        queries = qkv[block, pl.ds(2 * tile, 2), 0].reshape(q_tile, HD)
        scores = lax.dot_general(queries, keys, (((1,), (1,)), ((), ())), preferred_element_type=F32)
        weight = jnp.exp2(scores).astype(BF16)
        added = weight[:, :HD].astype(F32)
        for k in range(1, keys.shape[0] // HD):
            added = added + weight[:, k * HD : (k + 1) * HD].astype(F32)
        product = jnp.dot(weight, values, preferred_element_type=F32)
        if first:
            totals[here] = added
            acc[here] = product
        else:
            totals[here] += added
            acc[here] += product

    for tile in range(2):
        attend(True, text_k_ref[...], text_v_ref[...], tile)

    def step(t, carry):
        def at(n, work):
            @pl.when(t == n)
            def _():
                work()

        def mates(i, j):
            return lambda: kv_ring.landed(i, j, kv_mate)

        at(0, lambda: o_ring.forward(0, True))
        at(2, lambda: kv_ring.forward(0, True))
        at(2, mates(0, 2))
        at(2, mates(1, 2))
        at(3, mates(2, 2))
        at(3, mates(3, 2))
        at(4, lambda: kv_ring.forward(1, True))
        at(5, lambda: o_ring.forward(1, True))
        at(6, mates(0, 4))
        at(6, mates(1, 4))
        at(6, lambda: kv_ring.forward(2, True))
        at(7, mates(0, 6))
        at(7, mates(1, 6))
        at(8, lambda: kv_ring.forward(3, True))
        at(9, lambda: o_ring.opposite(0, True))
        at(9, lambda: kv_ring.opposite(0, True))
        at(10, mates(2, 4))
        at(10, mates(3, 4))
        at(10, lambda: kv_ring.opposite(1, True))
        at(11, mates(2, 6))
        at(11, mates(3, 6))
        at(11, lambda: kv_ring.opposite(2, True))
        at(12, lambda: kv_ring.opposite(3, True))
        at(12, lambda: o_ring.opposite(1, True))
        at(13, mates(0, 7))
        at(13, mates(1, 7))
        at(15, mates(2, 7))
        at(15, mates(3, 7))
        late = t >= 12
        wide = lax.rem(t, 4)
        place = jnp.where(t < 4, 0, jnp.where(late, 2, jnp.where(lax.rem(t, 2) == 0, 3, 1)))
        other = jnp.where(t < 4, lax.div(t, 2), jnp.where(late, lax.rem(t, 2), lax.div(wide, 2)))
        pair = jnp.where(t < 4, lax.rem(t, 2), jnp.where(late, lax.div(t - 12, 2), lax.div(t - 4, 4)))
        b = 2 * lax.rem(z + place, 4) + lax.rem(core + other, 2)
        first = 2 * xh + lax.rem(xl + pair, 2)
        second = 2 * (1 - xh) + lax.rem(xl + pair, 2)
        keys = jnp.concatenate([qkv[b, first, 1], qkv[b, second, 1]], axis=0)
        values = jnp.concatenate([qkv[b, first, 2], qkv[b, second, 2]], axis=0)
        for tile in range(2):
            attend(False, keys, values, tile)
        return carry

    lax.fori_loop(0, 16, step, 0)

    head = 2 * sp + xh

    def attended_copy(n):
        dx, dy = plane[n]
        source = 4 * lax.rem(x + dx, 4) + lax.rem(y + dy, 4)
        return pltpu.make_async_remote_copy(
            src_ref=att_out.at[source],
            dst_ref=att.at[:, pl.ds(pl.multiple_of(head * HD, HD), HD)],
            send_sem=at_send.at[n],
            recv_sem=at_recv.at[n],
            device_id=on_plane(dx, dy),
            device_id_type=MESH,
        )

    for s in range(4):
        here = pl.ds(s * keys_here, keys_here)
        total = jnp.sum(totals[here], axis=-1, keepdims=True)
        att_out[pl.ds(4 * s, 4)] = (acc[here] / total).astype(BF16).reshape(4, rows, HD)
    for n in range(len(plane)):
        attended_copy(n).start()
    att[:, pl.ds(pl.multiple_of(head * HD, HD), HD)] = att_out[4 * x + y]

    for j in (4, 6, 7):
        o_ring.landed(0, j, out_mate)
    for j in (2, 4, 6, 7):
        o_ring.landed(1, j, out_mate)
    for n, (dx, dy) in enumerate(plane):
        from_x, from_y = lax.rem(x + 4 - dx, 4), lax.rem(y + 4 - dy, 4)
        from_head = 2 * (2 * from_y + lax.rem(from_x, 2)) + lax.div(from_x, 2)
        slot = att.at[:, pl.ds(pl.multiple_of(from_head * HD, HD), HD)]
        pltpu.make_async_remote_copy(
            src_ref=slot,
            dst_ref=slot,
            send_sem=at_send.at[n],
            recv_sem=at_recv.at[n],
            device_id=on_plane(dx, dy),
            device_id_type=MESH,
        ).wait_recv()

    def project(n, carry):
        columns = pl.ds(pl.multiple_of(n * 512, 512), 512)
        proj = jnp.dot(att[...], w_out[:, columns], preferred_element_type=F32)
        out_ref[:, columns] = (x_ref[:, columns].astype(F32) + gate_ref[:, columns] * proj).astype(BF16)
        return carry

    lax.fori_loop(0, width // 512, project, 0)
    final = layer_norm(out_ref[...].astype(F32)).astype(BF16)
    latent = lax.dot_general(final, w_final_ref[...], (((1,), (1,)), ((), ())), preferred_element_type=F32)
    latent = latent.astype(BF16)

    frames, breadth = 2, rows // 2
    patch = latent.shape[1] // 2
    row, col = (lax.broadcasted_iota(jnp.int32, (rows, rows), d) for d in (0, 1))
    feature, lane = (lax.broadcasted_iota(jnp.int32, (2 * patch, HD), d) for d in (0, 1))
    same = lax.div(row, breadth) == lax.div(col, breadth)
    views = [jnp.zeros((rows, HD), F32)] * 2
    for d in range(3):
        shift = ((col == row + (d - 1)) & same).astype(F32).astype(BF16)
        moved = jnp.dot(shift, latent, preferred_element_type=F32).astype(BF16)
        for p in range(2):
            spread = (feature - p * patch == lane - d * patch) & (lane >= d * patch) & (lane < (d + 1) * patch)
            views[p] += jnp.dot(moved, spread.astype(F32).astype(BF16), preferred_element_type=F32)
    for p in range(2):
        for f in range(frames):
            lat_ref[f, p] = views[p][f * breadth : (f + 1) * breadth].astype(BF16)

    for i in range(3):
        weight_hop(i).wait_send()
        w_ring.finish(i, range(8))
        for a in range(2):
            far_copy(i, a).wait_send()
    t_ring.finish(0, (0, 1, 3, 5))
    out_hop(out_piece(0, y)).wait_send()
    o_ring.finish(0, (0, 1, 3, 4, 5, 6, 7))
    o_ring.finish(1, range(8))
    for j in range(4):
        near_copy(j, places[j], False).wait_send()
        kv_ring.finish(j, range(8))
    for n in range(len(plane)):
        attended_copy(n).wait_send()


def decode_kernel(lat_ref, w_in_ref, w_mid_ref, clip_ref, out_ref, window, w_taps, planes, direct, send, recv):
    grp, sp = lax.axis_index("grp"), lax.axis_index("sp")
    slabs, tiles = lax.axis_size("grp"), lax.axis_size("sp")
    breadth = lat_ref.shape[1] // 2
    cv = w_in_ref.shape[-1]
    ways = [(dg, ds) for dg in range(3) for ds in (-1, 0, 1) if dg or ds]

    def inside(dg, ds):
        g, s = grp + dg, sp + ds
        return (g >= 0) & (g < slabs) & (s >= 0) & (s < tiles)

    barrier = pltpu.get_barrier_semaphore()
    count = 0
    for dg in (-2, -1, 0, 1, 2):
        for ds in (-1, 0, 1):
            if dg or ds:
                there = inside(dg, ds)

                @pl.when(there)
                def _():
                    pl.semaphore_signal(barrier, inc=1, device_id=(grp + dg, sp + ds), device_id_type=MESH)

                count = count + jnp.where(there, 1, 0)

    @pl.when(sp == 0)
    def _():
        window[:, 0 : 2 * breadth] = jnp.zeros((6, 2 * breadth, HD), BF16)

    @pl.when(sp == tiles - 1)
    def _():
        window[:, 4 * breadth :] = jnp.zeros((6, 2 * breadth, HD), BF16)

    for first in (0, 1):

        @pl.when(grp == first)
        def _():
            window[0 : 4 - 2 * first] = jnp.zeros((4 - 2 * first, 6 * breadth, HD), BF16)

    pl.semaphore_wait(barrier, count)

    def halo_copy(n):
        dg, ds = ways[n]
        return pltpu.make_async_remote_copy(
            src_ref=lat_ref,
            dst_ref=window.at[pl.ds(4 - 2 * dg, 2), pl.ds(2 * breadth * (1 - ds), 2 * breadth)],
            send_sem=send.at[n],
            recv_sem=recv.at[n],
            device_id=(grp + dg, sp + ds),
            device_id_type=MESH,
        )

    for n, (dg, ds) in enumerate(ways):

        @pl.when(inside(dg, ds))
        def _():
            halo_copy(n).start()

    window[pl.ds(4, 2), pl.ds(2 * breadth, 2 * breadth)] = lat_ref[...]

    w_taps[...] = jnp.zeros_like(w_taps)
    ch = w_in_ref.shape[3]
    for kt in range(3):
        for kr in range(3):
            for d in range(3):
                for q in range(2):
                    for q_out in range(2):
                        kc = 2 * (d - 1) + q - q_out + 1
                        if 0 <= kc < 3:
                            w_taps[3 * kt + kr, pl.ds((2 * d + q) * ch, ch), pl.ds(cv * q_out, cv)] = w_in_ref[kt, kr, kc]

    first_frame = 2 * grp
    starts = []
    for f in range(4):
        clip = clip_ref[jnp.maximum(first_frame - 2 + f, 0)]
        start = 0
        for j in range(clip_ref.shape[0]):
            start = start + jnp.where(clip_ref[j] < clip, 1, 0)
        starts.append(start)

    for n, (dg, ds) in enumerate(ways):

        @pl.when(inside(-dg, -ds))
        def _():
            halo_copy(n).wait_recv()

    def frame_at(f, kt, lowest, size):
        index = jnp.maximum(first_frame - 2 + f - kt, starts[f]) - (first_frame - lowest)
        return jnp.clip(index, 0, size - 1)

    tile = lax.broadcasted_iota(jnp.int32, (4 * breadth, 1), 0)
    outside = ((tile < breadth) & (sp == 0)) | ((tile >= 3 * breadth) & (sp == tiles - 1))
    row, col = (lax.broadcasted_iota(jnp.int32, (4 * breadth, 4 * breadth), d) for d in (0, 1))
    same = lax.div(row, breadth) == lax.div(col, breadth)
    left = ((col == row - 1) & same).astype(F32).astype(BF16)
    right = ((col == row + 1) & same).astype(F32).astype(BF16)
    for f in range(4):
        total = jnp.zeros((4 * breadth, 2 * cv), F32)
        for kt in range(3):
            index = frame_at(f, kt, 4, 6)
            for kr in range(3):
                seen = window[index, pl.ds(kr * breadth, 4 * breadth)]
                total = total + jnp.dot(seen, w_taps[3 * kt + kr], preferred_element_type=F32)
        if f >= 2:
            direct[f - 2] = total[breadth : 3 * breadth]
        act = jnp.where(outside, 0.0, total / (1.0 + jnp.exp(-total))).astype(BF16)
        even, odd = act[:, :cv], act[:, cv:]
        planes[0, f] = jnp.dot(left, odd, preferred_element_type=F32).astype(BF16)
        planes[1, f] = even
        planes[2, f] = odd
        planes[3, f] = jnp.dot(right, even, preferred_element_type=F32).astype(BF16)

    mixed = jnp.zeros((8 * breadth, cv), F32)
    for kt in range(3):
        index = [frame_at(2 + f, kt, 2, 4) for f in range(2)]
        for kr in range(3):
            rows = pl.ds(kr * breadth, 2 * breadth)
            seen = [
                jnp.concatenate([planes[q + kc, index[f], rows] for kc in range(3)], axis=1)
                for f in range(2)
                for q in range(2)
            ]
            mixed = mixed + jnp.dot(jnp.concatenate(seen, axis=0), w_mid_ref[3 * kt + kr], preferred_element_type=F32)

    row, col = (lax.broadcasted_iota(jnp.int32, (2 * breadth, 2 * breadth), d) for d in (0, 1))
    woven = (col == lax.div(row, 2) + breadth * lax.rem(row, 2)).astype(F32).astype(BF16)
    for f in range(2):
        for r in range(2):
            pair = []
            for q in range(2):
                start = (2 * f + q) * 2 * breadth + r * breadth
                added = mixed[start : start + breadth] + direct[f, r * breadth : (r + 1) * breadth, q * cv : (q + 1) * cv]
                pair.append(added.astype(BF16))
            out_ref[f, r] = jnp.dot(woven, jnp.concatenate(pair, axis=0), preferred_element_type=F32).astype(BF16)

    for n, (dg, ds) in enumerate(ways):

        @pl.when(inside(dg, ds))
        def _():
            halo_copy(n).wait_send()


def per_device(
    image_tokens,
    text_tokens,
    mod_shift,
    mod_scale,
    mod_gate,
    w_qkv,
    w_text_kv,
    q_gain,
    k_gain,
    text_gain,
    w_out,
    w_final,
    w_conv_in,
    w_conv_mid,
    clip_ids,
):
    slab, patch_rows, breadth, width = image_tokens.shape
    rows = slab * patch_rows * breadth
    inner_here = w_qkv.shape[2]
    inner = w_out.shape[0] * lax.axis_size("sp")
    cv = w_conv_in.shape[-1]
    head_here = lax.rem(lax.div(lax.axis_index("grp"), 2), 2)
    text_count = text_tokens.shape[0]
    text_normed = layer_norm(text_tokens.astype(F32)).astype(BF16)
    w_text = lax.dynamic_slice_in_dim(w_text_kv, head_here * HD, HD, axis=2)
    text_projected = jnp.dot(text_normed, w_text.reshape(width, 2 * HD), preferred_element_type=F32)
    text_keys = rms_scale(text_projected[:, :HD], text_gain).astype(BF16)
    text_values = text_projected[:, HD:].astype(BF16)

    vmem = pl.BlockSpec(memory_space=pltpu.VMEM)
    anywhere = pl.BlockSpec(memory_space=pl.ANY)
    dma = pltpu.SemaphoreType.DMA
    block_flat, views = pl.pallas_call(
        block_kernel,
        out_shape=(
            jax.ShapeDtypeStruct((rows, width), BF16),
            jax.ShapeDtypeStruct((slab, 2, breadth, HD), BF16),
        ),
        in_specs=[vmem] * 4 + [anywhere] + [vmem] * 4 + [anywhere, vmem],
        out_specs=(vmem, vmem),
        scratch_shapes=[
            pltpu.VMEM((4, rows, width), BF16),
            pltpu.VMEM((2, 3, width, inner_here), BF16),
            pltpu.VMEM((8, 4, 3, 4 * rows, HD), BF16),
            pltpu.VMEM((4, 2, 3, rows, HD), BF16),
            pltpu.VMEM((3, 2, 4 * rows, HD), BF16),
            pltpu.VMEM((16 * rows, HD), F32),
            pltpu.VMEM((16 * rows, HD), F32),
            pltpu.VMEM((inner, width), BF16),
            pltpu.VMEM((16, rows, HD), BF16),
            pltpu.VMEM((rows, inner), BF16),
            dma((2,)),
            dma((4,)),
            dma((3,)),
            dma((3,)),
            dma((3, 8)),
            dma((3, 8)),
            dma((1, 8)),
            dma((1, 8)),
            dma((1,)),
            dma((1,)),
            dma((2, 8)),
            dma((2, 8)),
            dma((4,)),
            dma((4,)),
            dma((2, 3)),
            dma((2, 3)),
            dma((4, 8)),
            dma((4, 8)),
            dma((15,)),
            dma((15,)),
        ],
        compiler_params=pltpu.CompilerParams(
            collective_id=0, has_side_effects=True, vmem_limit_bytes=58 * 1024 * 1024
        ),
    )(
        image_tokens.reshape(rows, width),
        mod_shift.reshape(1, width),
        mod_scale.reshape(1, width),
        mod_gate.reshape(1, width),
        jnp.transpose(w_qkv, (1, 0, 2)),
        text_keys,
        text_values,
        q_gain.reshape(1, HD),
        k_gain.reshape(1, HD),
        w_out,
        jnp.transpose(w_final),
    )

    decoded = pl.pallas_call(
        decode_kernel,
        out_shape=jax.ShapeDtypeStruct((slab, 2 * patch_rows, 2 * breadth, cv), BF16),
        in_specs=[vmem] * 3 + [pl.BlockSpec(memory_space=pltpu.SMEM)],
        out_specs=vmem,
        scratch_shapes=[
            pltpu.VMEM((6, 6 * breadth, HD), BF16),
            pltpu.VMEM((9, HD, 2 * cv), BF16),
            pltpu.VMEM((4, 4, 4 * breadth, cv), BF16),
            pltpu.VMEM((2, 2 * breadth, 2 * cv), F32),
            dma((8,)),
            dma((8,)),
        ],
        compiler_params=pltpu.CompilerParams(
            collective_id=1, has_side_effects=True, vmem_limit_bytes=32 * 1024 * 1024
        ),
    )(
        views.reshape(slab, 2 * breadth, HD),
        w_conv_in,
        w_conv_mid.reshape(9, 3 * cv, cv),
        clip_ids,
    )
    return (block_flat.reshape(slab, patch_rows, breadth, width), decoded)


def solution(mesh):
    return jax.shard_map(
        per_device,
        mesh=mesh,
        in_specs=(
            P("grp", "sp", None, None),
            P(),
            P(),
            P(),
            P(),
            P(None, None, "sp"),
            P(None, None, "sp"),
            P(),
            P(),
            P(),
            P("sp", None),
            P(),
            P(),
            P(),
            P(),
        ),
        out_specs=(P("grp", "sp", None, None), P("grp", "sp", None, None)),
        check_vma=False,
    )
```

```python
import math

import jax
import jax.numpy as jnp
from jax import lax
from jax.experimental import pallas as pl
from jax.experimental.pallas import tpu as pltpu
from jax.sharding import PartitionSpec as P

HD = 128
EPS = 1e-06
MESH = pl.DeviceIdType.MESH
F32 = jnp.float32
BF16 = jnp.bfloat16


def layer_norm(values):
    middle = jnp.mean(values, axis=-1, keepdims=True)
    centered = values - middle
    spread = jnp.mean(centered * centered, axis=-1, keepdims=True)
    return centered * lax.rsqrt(spread + EPS)


def rms_scale(values, gain):
    return values * lax.rsqrt(jnp.mean(values * values, axis=-1, keepdims=True) + EPS) * gain


class Ring:
    def __init__(self, at, before, after, mate, piece, half, send, recv):
        self.at = at
        self.before, self.after, self.mate = before, after, mate
        self.piece, self.half = piece, half
        self.send, self.recv = send, recv

    def copy(self, i, slot, j, device):
        return pltpu.make_async_remote_copy(
            src_ref=slot,
            dst_ref=slot,
            send_sem=self.send.at[i, j],
            recv_sem=self.recv.at[i, j],
            device_id=device,
            device_id_type=MESH,
        )

    def place(self, step):
        return lax.rem(self.at + step, 4)

    def out(self, i, j):
        if j in (0, 1, 2):
            return self.copy(i, self.piece(i, self.at), j, (self.after, self.before, self.mate)[j])
        if j == 3:
            return self.copy(i, self.half(i, self.place(3), 0), j, self.after)
        if j == 5:
            return self.copy(i, self.half(i, self.place(1), 1), j, self.before)
        return self.copy(i, self.piece(i, self.place({4: 3, 6: 1, 7: 2}[j])), j, self.mate)

    def start(self, i, mate):
        for j in (0, 1, 2) if mate else (0, 1):
            self.out(i, j).start()

    def landed(self, i, j, mate_piece=None):
        slot = {
            0: lambda: self.piece(i, self.place(3)),
            1: lambda: self.piece(i, self.place(1)),
            3: lambda: self.half(i, self.place(2), 0),
            5: lambda: self.half(i, self.place(2), 1),
        }
        if j in slot:
            where = slot[j]()
        else:
            where = mate_piece(i, self.place({2: 0, 4: 3, 6: 1, 7: 2}[j]))
        self.copy(i, where, j, self.after).wait_recv()

    def forward(self, i, mate):
        self.landed(i, 0)
        self.out(i, 3).start()
        self.landed(i, 1)
        self.out(i, 5).start()
        if mate:
            self.out(i, 4).start()
            self.out(i, 6).start()

    def opposite(self, i, mate):
        self.landed(i, 3)
        self.landed(i, 5)
        if mate:
            self.out(i, 7).start()

    def finish(self, i, js):
        for j in js:
            self.out(i, j).wait_send()


def whole_kernel(
    x_ref,
    shift_ref,
    scale_ref,
    gate_ref,
    w_qkv_ref,
    text_ref,
    w_text_ref,
    q_gain_ref,
    k_gain_ref,
    text_gain_ref,
    w_out_ref,
    w_final_ref,
    w_in_ref,
    w_mid_ref,
    clip_ref,
    out_ref,
    dec_ref,
    tokens,
    weights,
    qkv,
    stage,
    relay,
    acc,
    totals,
    w_out,
    att_out,
    att,
    text,
    w_text,
    text_kv,
    lat,
    window,
    w_taps,
    planes,
    direct,
    local_sem,
    copy_sem,
    wx_send,
    wx_recv,
    w_send,
    w_recv,
    t_send,
    t_recv,
    o_send,
    o_recv,
    side_send,
    side_recv,
    over_send,
    over_recv,
    far_send,
    far_recv,
    relay_send,
    relay_recv,
    near_send,
    near_recv,
    kv_send,
    kv_recv,
    at_send,
    at_recv,
    halo_send,
    halo_recv,
):
    grp, sp = lax.axis_index("grp"), lax.axis_index("sp")
    z, xh, core = lax.div(grp, 4), lax.rem(lax.div(grp, 2), 2), lax.rem(grp, 2)
    y, xl = lax.div(sp, 2), lax.rem(sp, 2)
    x = 2 * xh + xl
    rows, width = x_ref.shape
    piece_rows = width // 8
    keys_here = 4 * rows
    out_half = width // 2

    def device(dz=0, dxh=0, dcore=0, dy=0, dxl=0):
        new_grp = 4 * lax.rem(z + dz, 4) + 2 * lax.rem(xh + dxh, 2) + lax.rem(core + dcore, 2)
        new_sp = 2 * lax.rem(y + dy, 4) + lax.rem(xl + dxl, 2)
        return (new_grp, new_sp)

    def flip(a, b):
        return device(dxh=a, dxl=b)

    own_weights = pltpu.make_async_copy(w_qkv_ref, weights.at[xl], local_sem.at[0])
    own_weights.start()
    text_in = pltpu.make_async_copy(text_ref, text, local_sem.at[1])
    text_in.start()
    w_text_in = pltpu.make_async_copy(w_text_ref, w_text, local_sem.at[2])
    w_text_in.start()
    out_rows = pl.ds(pl.multiple_of(256 * sp, 256), 256)
    own_out = pltpu.make_async_copy(w_out_ref, w_out.at[out_rows], local_sem.at[3])
    own_out.start()

    plane = [(a, b, dy) for a, b in ((1, 0), (0, 1), (1, 1), (0, 0)) for dy in (2, 1, 3, 0) if a or b or dy]

    def on_plane(a, b, dy):
        return device(dxh=a, dxl=b, dy=dy)

    slabs, tiles = lax.axis_size("grp"), lax.axis_size("sp")
    ways = [(dg, ds) for dg in range(3) for ds in (-1, 0, 1) if dg or ds]

    def inside(dg, ds):
        g, s = grp + dg, sp + ds
        return (g >= 0) & (g < slabs) & (s >= 0) & (s < tiles)

    barrier = pltpu.get_barrier_semaphore()
    partners = [device(dz=1), device(dz=3), device(dcore=1)] + [on_plane(*place) for place in plane]
    for partner in partners:
        pl.semaphore_signal(barrier, inc=1, device_id=partner, device_id_type=MESH)
    expected = len(partners)
    for dg in (-2, -1, 0, 1, 2):
        for ds in (-1, 0, 1):
            if dg or ds:
                there = inside(dg, ds)

                @pl.when(there)
                def _():
                    pl.semaphore_signal(barrier, inc=1, device_id=(grp + dg, sp + ds), device_id_type=MESH)

                expected = expected + jnp.where(there, 1, 0)

    breadth = rows // 2
    zero_rows = jnp.zeros((6, 2 * breadth, HD), BF16)

    @pl.when(sp == 0)
    def _():
        window[:, 0 : 2 * breadth] = zero_rows

    @pl.when(sp == tiles - 1)
    def _():
        window[:, 4 * breadth :] = zero_rows

    for first in (0, 1):

        @pl.when(grp == first)
        def _():
            window[0 : 4 - 2 * first] = jnp.zeros((4 - 2 * first, 6 * breadth, HD), BF16)

    pl.semaphore_wait(barrier, expected)

    def weight_rows(place, c):
        return pl.ds(pl.multiple_of(piece_rows * (2 * place + c), 128), piece_rows)

    def weight_piece(i, place):
        return weights.at[1 - xl, (1, 2, 0)[i], weight_rows(place, core)]

    def weight_half(i, place, h):
        start = piece_rows * (2 * place + core) + h * (piece_rows // 2)
        return weights.at[1 - xl, (1, 2, 0)[i], pl.ds(pl.multiple_of(start, 64), piece_rows // 2)]

    def weight_mate(i, place):
        return weights.at[1 - xl, (1, 2, 0)[i], weight_rows(place, 1 - core)]

    def weight_hop(i, a, landing=False):
        part = (1, 2, 0)[i]
        start = piece_rows * (2 * z + core) + a * (piece_rows // 2)
        here = pl.ds(pl.multiple_of(start, 64), piece_rows // 2)
        slot = weights.at[1 - xl if landing else xl, part, here]
        return pltpu.make_async_remote_copy(
            src_ref=slot if landing else w_qkv_ref.at[part, here],
            dst_ref=slot,
            send_sem=wx_send.at[i, a],
            recv_sem=wx_recv.at[i, a],
            device_id=flip(a, 1),
            device_id_type=MESH,
        )

    w_ring = Ring(z, device(dz=3), device(dz=1), device(dcore=1), weight_piece, weight_half, w_send, w_recv)

    def weight_landed(i):
        for a in range(2):
            weight_hop(i, a, True).wait_recv()

    t_before, t_after, t_far = lax.rem(y + 3, 4), lax.rem(y + 1, 4), lax.rem(y + 2, 4)

    def token_copy(n, landing=False):
        place = (t_before, t_after, t_before, t_after, t_far, t_far)[n] if landing else (y, y, y, y, t_before, t_after)[n]
        h = (0, 1, 1, 0, 0, 1)[n]
        slot = tokens.at[place, pl.ds(h * (rows // 2), rows // 2)]
        return pltpu.make_async_remote_copy(
            src_ref=slot,
            dst_ref=slot,
            send_sem=t_send.at[n],
            recv_sem=t_recv.at[n],
            device_id=device(dy=(1, 3, 1, 3, 1, 3)[n]),
            device_id_type=MESH,
        )

    for i in range(3):
        for a in range(2):
            weight_hop(i, a).start()
    for h in range(2):
        here = pl.ds(h * (rows // 2), rows // 2)
        normed = layer_norm(x_ref[here].astype(F32)) * (1.0 + scale_ref[...]) + shift_ref[...]
        tokens[y, here] = normed.astype(BF16)
        token_copy(h).start()
    token_copy(2).start()
    token_copy(3).start()

    places = [y, t_before, t_after, t_far]

    def out_slot(sp_of, h, c):
        start, count = (256 * sp_of, 256) if h is None else (256 * sp_of + 128 * h, 128)
        columns = pl.ds(pl.multiple_of(out_half * c, 128), out_half)
        return w_out.at[pl.ds(pl.multiple_of(start, 128), count), columns]

    def out_piece(i, place):
        return out_slot(2 * place + xl, None, core)

    def out_mate(i, place):
        return out_slot(2 * place + xl, None, 1 - core)

    def out_half_of(i, place, h):
        return out_slot(2 * place + xl, h, core)

    o_ring = Ring(y, device(dy=3), device(dy=1), device(dcore=1), out_piece, out_half_of, o_send, o_recv)

    def side_copy(n, a, landing=False):
        slot = out_slot(2 * places[n] + (1 - xl if landing else xl), a, core)
        return pltpu.make_async_remote_copy(
            src_ref=slot,
            dst_ref=slot,
            send_sem=side_send.at[n, a],
            recv_sem=side_recv.at[n, a],
            device_id=flip(a, 1),
            device_id_type=MESH,
        )

    def over_copy(n, landing=False):
        slot = out_slot(2 * places[n] + 1 - xl, None, 1 - core if landing else core)
        return pltpu.make_async_remote_copy(
            src_ref=slot,
            dst_ref=slot,
            send_sem=over_send.at[n],
            recv_sem=over_recv.at[n],
            device_id=device(dcore=1),
            device_id_type=MESH,
        )

    def send_sideways(n):
        for a in range(2):
            side_copy(n, a).start()

    def send_over(n):
        for a in range(2):
            side_copy(n, a, True).wait_recv()
        over_copy(n).start()

    scale = HD ** (-0.5) / math.log(2.0)
    q_gain = q_gain_ref[...] * scale
    k_gain = k_gain_ref[...]
    block = 2 * z + core

    def finish_part(part, values):
        if part == 2:
            return values.astype(BF16)
        return rms_scale(values, q_gain if part == 0 else k_gain).astype(BF16)

    def token_rows(j):
        return pl.ds(pl.multiple_of(places[j] * rows, rows), rows)

    def own_copy(j):
        return pltpu.make_async_copy(stage.at[0, j, xh], qkv.at[block, x, :, token_rows(j)], copy_sem.at[j])

    def far_copy(a, j, part, landing=False):
        source = 2 * lax.rem(xh + a, 2) + 1 - xl if landing else x
        slot = qkv.at[block, source, part, token_rows(j)]
        return pltpu.make_async_remote_copy(
            src_ref=slot if landing else stage.at[1, j, lax.rem(xh + a, 2), part],
            dst_ref=slot,
            send_sem=far_send.at[a, j, part],
            recv_sem=far_recv.at[a, j, part],
            device_id=flip(a, 1),
            device_id_type=MESH,
        )

    def relay_copy(j, landing=False):
        return pltpu.make_async_remote_copy(
            src_ref=relay.at[j] if landing else stage.at[0, j, 1 - xh],
            dst_ref=relay.at[j],
            send_sem=relay_send.at[j],
            recv_sem=relay_recv.at[j],
            device_id=flip(j % 2, 1),
            device_id_type=MESH,
        )

    def near_copy(j, landing=False):
        source = 2 * (1 - xh) + xl if landing else 2 * lax.rem(xh + j % 2, 2) + 1 - xl
        slot = qkv.at[block, source, :, token_rows(j)]
        return pltpu.make_async_remote_copy(
            src_ref=slot if landing else relay.at[j],
            dst_ref=slot,
            send_sem=near_send.at[j],
            recv_sem=near_recv.at[j],
            device_id=flip(1 - j % 2, 1),
            device_id_type=MESH,
        )

    def hand_on(j):
        relay_copy(j, True).wait_recv()
        near_copy(j).start()

    def heads(b, js, parts):
        seen = jnp.concatenate([tokens[places[j]] for j in js], axis=0)
        for part in parts:
            made = jnp.dot(seen, weights[lax.rem(xl + b, 2), part], preferred_element_type=F32)
            for head in range(2):
                done = finish_part(part, made[:, head * HD : (head + 1) * HD])
                for n, j in enumerate(js):
                    stage[b, j, head, part] = done[n * rows : (n + 1) * rows]
            if b == 1:
                for j in js:
                    for a in range(2):
                        far_copy(a, j, part).start()
        if b == 0:
            for j in js:
                relay_copy(j).start()
                own_copy(j).start()

    every = (1, 2, 0)

    def far_heads(i, js):
        for j in (2, 4, 6, 7):
            w_ring.landed(i, j, weight_mate)
        heads(1, js, every[i : i + 1])

    for i in range(3):
        weight_landed(i)
        w_ring.start(i, True)
    own_weights.wait()
    heads(0, [0], every)
    w_ring.forward(0, True)
    own_out.wait()
    send_sideways(0)
    hand_on(0)

    text_in.wait()
    w_text_in.wait()
    text_normed = layer_norm(text[...].astype(F32)).astype(BF16)
    text_made = jnp.dot(text_normed, w_text[...], preferred_element_type=F32)
    text_kv[0] = rms_scale(text_made[:, :HD], text_gain_ref[...]).astype(BF16)
    text_kv[1] = text_made[:, HD:].astype(BF16)

    token_copy(0, True).wait_recv()
    token_copy(4).start()
    token_copy(1, True).wait_recv()
    token_copy(5).start()
    w_ring.forward(1, True)
    w_ring.opposite(0, True)

    w_taps[...] = jnp.zeros_like(w_taps)
    ch, cv = w_in_ref.shape[3], w_in_ref.shape[4]
    for kt in range(3):
        for kr in range(3):
            for d in range(3):
                for q in range(2):
                    for q_out in range(2):
                        kc = 2 * (d - 1) + q - q_out + 1
                        if 0 <= kc < 3:
                            first = (3 * kt + kr) * HD + (2 * d + q) * ch
                            w_taps[pl.ds(first, ch), pl.ds(cv * q_out, cv)] = w_in_ref[kt, kr, kc]

    w_ring.forward(2, True)
    token_copy(2, True).wait_recv()
    token_copy(3, True).wait_recv()
    heads(0, [1, 2], every)
    w_ring.opposite(1, True)
    far_heads(0, [0, 1, 2])
    w_ring.opposite(2, True)
    hand_on(1)
    hand_on(2)
    far_heads(1, [0, 1, 2])
    token_copy(4, True).wait_recv()
    token_copy(5, True).wait_recv()
    o_ring.start(0, False)
    heads(0, [3], every)
    heads(1, [3], (1, 2))
    hand_on(3)
    far_heads(2, [0, 1, 2, 3])

    sources = [2 * lax.rem(xh + a, 2) + lax.rem(xl + b, 2) for b in range(2) for a in range(2)]

    def kv_piece_of(i, place, c):
        return qkv.at[2 * place + c, sources[i], pl.ds(1, 2)]

    def kv_piece(i, place):
        return kv_piece_of(i, place, core)

    def kv_half(i, place, h):
        return qkv.at[2 * place + core, sources[i], 1 + h]

    def kv_mate(i, place):
        return kv_piece_of(i, place, 1 - core)

    kv_ring = Ring(z, device(dz=3), device(dz=1), device(dcore=1), kv_piece, kv_half, kv_send, kv_recv)

    for j in range(4):
        own_copy(j).wait()
    kv_ring.start(0, True)
    for j in range(4):
        near_copy(j, True).wait_recv()
    kv_ring.start(1, True)
    for a in range(2):
        for j in range(4):
            for part in range(3):
                far_copy(a, j, part, True).wait_recv()
        kv_ring.start(2 + a, True)

    for i in range(3):
        w_ring.finish(i, range(8))
    w_mid = weights.at[0, :, pl.ds(0, w_mid_ref.shape[1])]
    w_mid_in = pltpu.make_async_copy(w_mid_ref, w_mid, local_sem.at[4])
    w_mid_in.start()

    q_tile = 2 * keys_here

    def attend(first, keys, values, tile):
        here = pl.ds(tile * q_tile if isinstance(tile, int) else pl.multiple_of(tile * q_tile, q_tile), q_tile)
        one = 2 * (1 - xh) + lax.rem(xl + tile, 2)
        two = 2 * xh + lax.rem(xl + 1 - tile, 2)
        queries = jnp.concatenate([qkv[block, one, 0], qkv[block, two, 0]], axis=0)
        scores = lax.dot_general(queries, keys, (((1,), (1,)), ((), ())), preferred_element_type=F32)
        weight = jnp.exp2(scores).astype(BF16)
        added = weight[:, :HD].astype(F32)
        for k in range(1, keys.shape[0] // HD):
            added = added + weight[:, k * HD : (k + 1) * HD].astype(F32)
        product = jnp.dot(weight, values, preferred_element_type=F32)
        if first:
            totals[here] = added
            acc[here] = product
        else:
            totals[here] += added
            acc[here] += product

    for tile in range(2):
        attend(True, text_kv[0], text_kv[1], tile)

    def chunk_pair(place, other, pair):
        b = 2 * lax.rem(z + place, 4) + lax.rem(core + other, 2)
        first = 2 * xh + lax.rem(xl + pair, 2)
        second = 2 * (1 - xh) + lax.rem(xl + pair, 2)
        keys = jnp.concatenate([qkv[b, first, 1], qkv[b, second, 1]], axis=0)
        values = jnp.concatenate([qkv[b, first, 2], qkv[b, second, 2]], axis=0)
        return keys, values

    def mates(i, j):
        return lambda: kv_ring.landed(i, j, kv_mate)

    def out_along():
        o_ring.forward(0, True)
        send_sideways(1)
        send_sideways(2)

    def out_opposite():
        o_ring.opposite(0, True)
        send_sideways(3)

    def step(t, carry):
        def at(n, work):
            @pl.when(t == n)
            def _():
                work()

        at(1, out_along)
        at(2, lambda: send_over(0))
        at(5, out_opposite)
        at(8, lambda: send_over(1))
        at(9, lambda: send_over(2))
        at(11, lambda: send_over(3))
        at(2, lambda: kv_ring.forward(0, True))
        at(2, mates(0, 2))
        at(2, mates(1, 2))
        at(3, mates(2, 2))
        at(3, mates(3, 2))
        at(4, lambda: kv_ring.forward(1, True))
        at(6, mates(0, 4))
        at(6, mates(1, 4))
        at(6, lambda: kv_ring.forward(2, True))
        at(7, mates(0, 6))
        at(7, mates(1, 6))
        at(8, lambda: kv_ring.forward(3, True))
        at(9, lambda: kv_ring.opposite(0, True))
        at(10, mates(2, 4))
        at(10, mates(3, 4))
        at(10, lambda: kv_ring.opposite(1, True))
        at(11, mates(2, 6))
        at(11, mates(3, 6))
        at(11, lambda: kv_ring.opposite(2, True))
        own = t < 4
        place = jnp.where(own, 0, jnp.where(lax.rem(t, 2) == 0, 3, 1))
        other = jnp.where(own, lax.div(t, 2), lax.div(lax.rem(t, 4), 2))
        pair = jnp.where(own, lax.rem(t, 2), lax.div(t - 4, 4))
        keys, values = chunk_pair(place, other, pair)
        for tile in range(2):
            attend(False, keys, values, tile)
        return carry

    lax.fori_loop(0, 12, step, 0)

    def last_step(pair, tile):
        if tile == 0:

            @pl.when(pair == 0)
            def _():
                mates(0, 7)()
                mates(1, 7)()
                kv_ring.opposite(3, True)

            @pl.when(pair == 1)
            def _():
                mates(2, 7)()
                mates(3, 7)()

        for other in range(2):
            keys, values = chunk_pair(2, other, pair)
            attend(False, keys, values, tile)

    head = 2 * sp + xh

    def attended_copy(n, landing=False):
        a, b, dy = plane[n]
        at_head = head
        if landing:
            from_sp = 2 * lax.rem(y + 4 - dy, 4) + lax.rem(xl + b, 2)
            at_head = 2 * from_sp + lax.rem(xh + a, 2)
        slot = att.at[:, pl.ds(pl.multiple_of(at_head * HD, HD), HD)]
        made = slot if landing else att_out.at[((1, 0), (0, 1), (1, 1), (0, 0)).index((a, b)), lax.rem(y + dy, 4)]
        return pltpu.make_async_remote_copy(
            src_ref=made,
            dst_ref=slot,
            send_sem=at_send.at[n],
            recv_sem=at_recv.at[n],
            device_id=on_plane(a, b, dy),
            device_id_type=MESH,
        )

    for tile in range(2):
        lax.fori_loop(0, 2, lambda pair, carry: last_step(pair, tile) or carry, 0)
        for r in (2 * tile, 2 * tile + 1):
            here = pl.ds(r * keys_here, keys_here)
            total = jnp.sum(totals[here], axis=-1, keepdims=True)
            att_out[r] = (acc[here] / total).astype(BF16).reshape(4, rows, HD)
            for n in range(4 * r, min(4 * r + 4, len(plane))):
                attended_copy(n).start()
    att[:, pl.ds(pl.multiple_of(head * HD, HD), HD)] = att_out[3, y]

    for j in (4, 6, 7):
        o_ring.landed(0, j, out_mate)
    for n in range(4):
        over_copy(n, True).wait_recv()
    for n in range(len(plane)):
        attended_copy(n, True).wait_recv()

    def project(n, carry):
        columns = pl.ds(pl.multiple_of(n * 512, 512), 512)
        proj = jnp.dot(att[...], w_out[:, columns], preferred_element_type=F32)
        out_ref[:, columns] = (x_ref[:, columns].astype(F32) + gate_ref[:, columns] * proj).astype(BF16)
        return carry

    lax.fori_loop(0, width // 512, project, 0)
    final = layer_norm(out_ref[...].astype(F32)).astype(BF16)
    latent = lax.dot_general(final, w_final_ref[...], (((1,), (1,)), ((), ())), preferred_element_type=F32)
    latent = latent.astype(BF16)

    patch = latent.shape[1] // 2
    row, col = (lax.broadcasted_iota(jnp.int32, (rows, rows), d) for d in (0, 1))
    feature, lane = (lax.broadcasted_iota(jnp.int32, (2 * patch, HD), d) for d in (0, 1))
    same = lax.div(row, breadth) == lax.div(col, breadth)
    views = [jnp.zeros((rows, HD), F32)] * 2
    for d in range(3):
        shift = ((col == row + (d - 1)) & same).astype(F32).astype(BF16)
        moved = jnp.dot(shift, latent, preferred_element_type=F32).astype(BF16)
        for p in range(2):
            spread = (feature - p * patch == lane - d * patch) & (lane >= d * patch) & (lane < (d + 1) * patch)
            views[p] += jnp.dot(moved, spread.astype(F32).astype(BF16), preferred_element_type=F32)
    for p in range(2):
        for f in range(2):
            lat[f, pl.ds(p * breadth, breadth)] = views[p][f * breadth : (f + 1) * breadth].astype(BF16)

    def halo_copy(n):
        dg, ds = ways[n]
        return pltpu.make_async_remote_copy(
            src_ref=lat,
            dst_ref=window.at[pl.ds(4 - 2 * dg, 2), pl.ds(2 * breadth * (1 - ds), 2 * breadth)],
            send_sem=halo_send.at[n],
            recv_sem=halo_recv.at[n],
            device_id=(grp + dg, sp + ds),
            device_id_type=MESH,
        )

    for n, (dg, ds) in enumerate(ways):

        @pl.when(inside(dg, ds))
        def _():
            halo_copy(n).start()

    window[pl.ds(4, 2), pl.ds(2 * breadth, 2 * breadth)] = lat[...]

    first_frame = 2 * grp
    starts = []
    for f in range(4):
        clip = clip_ref[jnp.maximum(first_frame - 2 + f, 0)]
        start = 0
        for j in range(clip_ref.shape[0]):
            start = start + jnp.where(clip_ref[j] < clip, 1, 0)
        starts.append(start)

    for n, (dg, ds) in enumerate(ways):

        @pl.when(inside(-dg, -ds))
        def _():
            halo_copy(n).wait_recv()

    def frame_at(f, kt, lowest, size):
        index = jnp.maximum(first_frame - 2 + f - kt, starts[f]) - (first_frame - lowest)
        return jnp.clip(index, 0, size - 1)

    tile = lax.broadcasted_iota(jnp.int32, (4 * breadth, 1), 0)
    outside = ((tile < breadth) & (sp == 0)) | ((tile >= 3 * breadth) & (sp == tiles - 1))
    row, col = (lax.broadcasted_iota(jnp.int32, (4 * breadth, 4 * breadth), d) for d in (0, 1))
    same = lax.div(row, breadth) == lax.div(col, breadth)
    left = ((col == row - 1) & same).astype(F32).astype(BF16)
    right = ((col == row + 1) & same).astype(F32).astype(BF16)
    for f in range(4):
        seen = []
        for kt in range(3):
            index = frame_at(f, kt, 4, 6)
            seen += [window[index, pl.ds(kr * breadth, 4 * breadth)] for kr in range(3)]
        total = jnp.dot(jnp.concatenate(seen, axis=1), w_taps[...], preferred_element_type=F32)
        if f >= 2:
            direct[f - 2] = total[breadth : 3 * breadth]
        act = jnp.where(outside, 0.0, total / (1.0 + jnp.exp(-total))).astype(BF16)
        even, odd = act[:, :cv], act[:, cv:]
        planes[0, f] = jnp.dot(left, odd, preferred_element_type=F32).astype(BF16)
        planes[1, f] = even
        planes[2, f] = odd
        planes[3, f] = jnp.dot(right, even, preferred_element_type=F32).astype(BF16)

    w_mid_in.wait()
    mixed = jnp.zeros((8 * breadth, cv), F32)
    for kt in range(3):
        index = [frame_at(2 + f, kt, 2, 4) for f in range(2)]
        for kr in range(3):
            here = pl.ds(kr * breadth, 2 * breadth)
            seen = [
                jnp.concatenate([planes[q + kc, index[f], here] for kc in range(3)], axis=1)
                for f in range(2)
                for q in range(2)
            ]
            taps = weights[0, kt, pl.ds(3 * cv * kr, 3 * cv)]
            mixed = mixed + jnp.dot(jnp.concatenate(seen, axis=0), taps, preferred_element_type=F32)

    row, col = (lax.broadcasted_iota(jnp.int32, (2 * breadth, 2 * breadth), d) for d in (0, 1))
    woven = (col == lax.div(row, 2) + breadth * lax.rem(row, 2)).astype(F32).astype(BF16)
    for f in range(2):
        for r in range(2):
            pair = []
            for q in range(2):
                start = (2 * f + q) * 2 * breadth + r * breadth
                added = mixed[start : start + breadth] + direct[f, r * breadth : (r + 1) * breadth, q * cv : (q + 1) * cv]
                pair.append(added.astype(BF16))
            dec_ref[f, r] = jnp.dot(woven, jnp.concatenate(pair, axis=0), preferred_element_type=F32).astype(BF16)

    for i in range(3):
        for a in range(2):
            weight_hop(i, a).wait_send()
    for n in range(6):
        token_copy(n).wait_send()
    o_ring.finish(0, (0, 1, 3, 4, 5, 6, 7))
    for j in range(4):
        relay_copy(j).wait_send()
        near_copy(j).wait_send()
        over_copy(j).wait_send()
        for a in range(2):
            side_copy(j, a).wait_send()
            for part in range(3):
                far_copy(a, j, part).wait_send()
        kv_ring.finish(j, range(8))
    for n in range(len(plane)):
        attended_copy(n).wait_send()
    for n, (dg, ds) in enumerate(ways):

        @pl.when(inside(dg, ds))
        def _():
            halo_copy(n).wait_send()


def per_device(
    image_tokens,
    text_tokens,
    mod_shift,
    mod_scale,
    mod_gate,
    w_qkv,
    w_text_kv,
    q_gain,
    k_gain,
    text_gain,
    w_out,
    w_final,
    w_conv_in,
    w_conv_mid,
    clip_ids,
):
    slab, patch_rows, breadth, width = image_tokens.shape
    rows = slab * patch_rows * breadth
    inner_here = w_qkv.shape[2]
    inner = w_out.shape[0] * lax.axis_size("sp")
    cv = w_conv_in.shape[-1]
    head_here = lax.rem(lax.div(lax.axis_index("grp"), 2), 2)
    text_count = text_tokens.shape[0]
    w_text = lax.dynamic_slice_in_dim(w_text_kv, head_here * HD, HD, axis=2).reshape(width, 2 * HD)

    vmem = pl.BlockSpec(memory_space=pltpu.VMEM)
    anywhere = pl.BlockSpec(memory_space=pl.ANY)
    dma = pltpu.SemaphoreType.DMA
    block_flat, decoded = pl.pallas_call(
        whole_kernel,
        out_shape=(
            jax.ShapeDtypeStruct((rows, width), BF16),
            jax.ShapeDtypeStruct((slab, 2 * patch_rows, 2 * breadth, cv), BF16),
        ),
        in_specs=[vmem] * 4
        + [anywhere] * 3
        + [vmem] * 3
        + [anywhere, vmem, vmem, anywhere, pl.BlockSpec(memory_space=pltpu.SMEM)],
        out_specs=(vmem, vmem),
        scratch_shapes=[
            pltpu.VMEM((4, rows, width), BF16),
            pltpu.VMEM((2, 3, width, inner_here), BF16),
            pltpu.VMEM((8, 4, 3, 4 * rows, HD), BF16),
            pltpu.VMEM((2, 4, 2, 3, rows, HD), BF16),
            pltpu.VMEM((4, 3, rows, HD), BF16),
            pltpu.VMEM((16 * rows, HD), F32),
            pltpu.VMEM((16 * rows, HD), F32),
            pltpu.VMEM((inner, width), BF16),
            pltpu.VMEM((4, 4, rows, HD), BF16),
            pltpu.VMEM((rows, inner), BF16),
            pltpu.VMEM((text_count, width), BF16),
            pltpu.VMEM((width, 2 * HD), BF16),
            pltpu.VMEM((2, text_count, HD), BF16),
            pltpu.VMEM((2, 2 * breadth, HD), BF16),
            pltpu.VMEM((6, 6 * breadth, HD), BF16),
            pltpu.VMEM((9 * HD, 2 * cv), BF16),
            pltpu.VMEM((4, 4, 4 * breadth, cv), BF16),
            pltpu.VMEM((2, 2 * breadth, 2 * cv), F32),
            dma((5,)),
            dma((4,)),
            dma((3, 2)),
            dma((3, 2)),
            dma((3, 8)),
            dma((3, 8)),
            dma((6,)),
            dma((6,)),
            dma((1, 8)),
            dma((1, 8)),
            dma((4, 2)),
            dma((4, 2)),
            dma((4,)),
            dma((4,)),
            dma((2, 4, 3)),
            dma((2, 4, 3)),
            dma((4,)),
            dma((4,)),
            dma((4,)),
            dma((4,)),
            dma((4, 8)),
            dma((4, 8)),
            dma((15,)),
            dma((15,)),
            dma((8,)),
            dma((8,)),
        ],
        compiler_params=pltpu.CompilerParams(
            collective_id=0, has_side_effects=True, vmem_limit_bytes=60 * 1024 * 1024
        ),
    )(
        image_tokens.reshape(rows, width),
        mod_shift.reshape(1, width),
        mod_scale.reshape(1, width),
        mod_gate.reshape(1, width),
        jnp.transpose(w_qkv, (1, 0, 2)),
        text_tokens,
        w_text,
        q_gain.reshape(1, HD),
        k_gain.reshape(1, HD),
        text_gain.reshape(1, HD),
        w_out,
        jnp.transpose(w_final),
        w_conv_in,
        w_conv_mid.reshape(3, 9 * cv, cv),
        clip_ids,
    )
    return (block_flat.reshape(slab, patch_rows, breadth, width), decoded)


def solution(mesh):
    return jax.shard_map(
        per_device,
        mesh=mesh,
        in_specs=(
            P("grp", "sp", None, None),
            P(),
            P(),
            P(),
            P(),
            P(None, None, "sp"),
            P(None, None, "sp"),
            P(),
            P(),
            P(),
            P("sp", None),
            P(),
            P(),
            P(),
            P(),
        ),
        out_specs=(P("grp", "sp", None, None), P("grp", "sp", None, None)),
        check_vma=False,
    )
```

```python
import functools
import math

import jax
import jax.numpy as jnp
from jax import lax
from jax.experimental import pallas as pl
from jax.experimental.pallas import tpu as pltpu
from jax.sharding import PartitionSpec as P

HD = 128
EPS = 1e-06
MESH = pl.DeviceIdType.MESH
F32 = jnp.float32
BF16 = jnp.bfloat16


def layer_norm(values):
    middle = jnp.mean(values, axis=-1, keepdims=True)
    centered = values - middle
    spread = jnp.mean(centered * centered, axis=-1, keepdims=True)
    return centered * lax.rsqrt(spread + EPS)


def rms_scale(values, gain):
    return values * lax.rsqrt(jnp.mean(values * values, axis=-1, keepdims=True) + EPS) * gain


class Ring:
    def __init__(self, at, before, after, mate, piece, half, send, recv):
        self.at = at
        self.before, self.after, self.mate = before, after, mate
        self.piece, self.half = piece, half
        self.send, self.recv = send, recv

    def copy(self, i, slot, j, device):
        return pltpu.make_async_remote_copy(
            src_ref=slot,
            dst_ref=slot,
            send_sem=self.send.at[i, j],
            recv_sem=self.recv.at[i, j],
            device_id=device,
            device_id_type=MESH,
        )

    def place(self, step):
        return lax.rem(self.at + step, 4)

    def out(self, i, j):
        if j in (0, 1, 2):
            return self.copy(i, self.piece(i, self.at), j, (self.after, self.before, self.mate)[j])
        if j == 3:
            return self.copy(i, self.half(i, self.place(3), 0), j, self.after)
        if j == 5:
            return self.copy(i, self.half(i, self.place(1), 1), j, self.before)
        return self.copy(i, self.piece(i, self.place({4: 3, 6: 1, 7: 2}[j])), j, self.mate)

    def start(self, i, mate):
        for j in (0, 1, 2) if mate else (0, 1):
            self.out(i, j).start()

    def landed(self, i, j, mate_piece=None):
        slot = {
            0: lambda: self.piece(i, self.place(3)),
            1: lambda: self.piece(i, self.place(1)),
            3: lambda: self.half(i, self.place(2), 0),
            5: lambda: self.half(i, self.place(2), 1),
        }
        if j in slot:
            where = slot[j]()
        else:
            where = mate_piece(i, self.place({2: 0, 4: 3, 6: 1, 7: 2}[j]))
        self.copy(i, where, j, self.after).wait_recv()

    def forward(self, i, mate):
        self.landed(i, 0)
        self.out(i, 3).start()
        self.landed(i, 1)
        self.out(i, 5).start()
        if mate:
            self.out(i, 4).start()
            self.out(i, 6).start()

    def opposite(self, i, mate):
        self.landed(i, 3)
        self.landed(i, 5)
        if mate:
            self.out(i, 7).start()

    def finish(self, i, js):
        for j in js:
            self.out(i, j).wait_send()


def whole_kernel(
    x_ref,
    shift_ref,
    scale_ref,
    gate_ref,
    w_qkv_ref,
    text_ref,
    w_text_ref,
    q_gain_ref,
    k_gain_ref,
    text_gain_ref,
    w_out_ref,
    w_final_ref,
    w_in_ref,
    w_mid_ref,
    clip_ref,
    out_ref,
    dec_ref,
    tokens,
    weights,
    qkv,
    stage,
    acc,
    totals,
    w_out,
    att_out,
    att,
    sums,
    text,
    w_text_raw,
    w_text,
    text_kv,
    lat,
    window,
    w_taps,
    planes,
    direct,
    local_sem,
    copy_sem,
    wx_send,
    wx_recv,
    wz_send,
    wz_recv,
    wo_send,
    wo_recv,
    t_send,
    t_recv,
    o_send,
    o_recv,
    side_send,
    side_recv,
    over_send,
    over_recv,
    far_send,
    far_recv,
    near_send,
    near_recv,
    kv_send,
    kv_recv,
    at_send,
    at_recv,
    halo_send,
    halo_recv,
):
    grp, sp = lax.axis_index("grp"), lax.axis_index("sp")
    z, xh, core = lax.div(grp, 4), lax.rem(lax.div(grp, 2), 2), lax.rem(grp, 2)
    y, xl = lax.div(sp, 2), lax.rem(sp, 2)
    x = 2 * xh + xl
    rows, width = x_ref.shape
    keys_here = 4 * rows
    out_half = width // 2

    def device(dz=0, dxh=0, dcore=0, dy=0, dxl=0):
        new_grp = 4 * lax.rem(z + dz, 4) + 2 * lax.rem(xh + dxh, 2) + lax.rem(core + dcore, 2)
        new_sp = 2 * lax.rem(y + dy, 4) + lax.rem(xl + dxl, 2)
        return (new_grp, new_sp)

    def flip(a, b):
        return device(dxh=a, dxl=b)

    own_weights = pltpu.make_async_copy(w_qkv_ref, weights.at[xl], local_sem.at[0])
    own_weights.start()
    text_in = pltpu.make_async_copy(text_ref, text, local_sem.at[1])
    text_in.start()
    w_text_in = pltpu.make_async_copy(w_text_ref, w_text_raw, local_sem.at[2])
    w_text_in.start()
    out_rows = pl.ds(pl.multiple_of(256 * sp, 256), 256)
    own_out = pltpu.make_async_copy(w_out_ref, w_out.at[out_rows], local_sem.at[3])
    own_out.start()

    plane = [(a, b, dy) for a, b in ((1, 0), (0, 1), (1, 1), (0, 0)) for dy in (2, 1, 3, 0) if a or b or dy]

    def on_plane(a, b, dy):
        return device(dxh=a, dxl=b, dy=dy)

    slabs, tiles = lax.axis_size("grp"), lax.axis_size("sp")
    ways = [(dg, ds) for dg in range(3) for ds in (-1, 0, 1) if dg or ds]

    def inside(dg, ds):
        g, s = grp + dg, sp + ds
        return (g >= 0) & (g < slabs) & (s >= 0) & (s < tiles)

    barrier = pltpu.get_barrier_semaphore()
    partners = [device(dz=1), device(dz=3), device(dcore=1)] + [on_plane(*place) for place in plane]
    for partner in partners:
        pl.semaphore_signal(barrier, inc=1, device_id=partner, device_id_type=MESH)
    expected = len(partners)
    for dg in (-2, -1, 0, 1, 2):
        for ds in (-1, 0, 1):
            if dg or ds:
                there = inside(dg, ds)

                @pl.when(there)
                def _():
                    pl.semaphore_signal(barrier, inc=1, device_id=(grp + dg, sp + ds), device_id_type=MESH)

                expected = expected + jnp.where(there, 1, 0)

    breadth = rows // 2
    zero_rows = jnp.zeros((6, 2 * breadth, HD), BF16)

    @pl.when(sp == 0)
    def _():
        window[:, 0 : 2 * breadth] = zero_rows

    @pl.when(sp == tiles - 1)
    def _():
        window[:, 4 * breadth :] = zero_rows

    for first in (0, 1):

        @pl.when(grp == first)
        def _():
            window[0 : 4 - 2 * first] = jnp.zeros((4 - 2 * first, 6 * breadth, HD), BF16)

    pl.semaphore_wait(barrier, expected)

    eighth = width // 8
    every = (1, 2, 0)

    def weight_slot(i, half, c, first, count):
        start = eighth * (4 * half + 2 * c + first)
        return (every[i], pl.ds(pl.multiple_of(start, eighth), eighth * count))

    parity = lax.rem(z, 2)

    def weight_hop(i, a, landing=False):
        here = weight_slot(i, parity, core, a, 1)
        slot = weights.at[(1 - xl if landing else xl,) + here]
        return pltpu.make_async_remote_copy(
            src_ref=slot if landing else w_qkv_ref.at[here],
            dst_ref=slot,
            send_sem=wx_send.at[i, a],
            recv_sem=wx_recv.at[i, a],
            device_id=flip(a, 1),
            device_id_type=MESH,
        )

    def weight_along(i, a, landing=False):
        slot = weights.at[(1 - xl,) + weight_slot(i, 1 - parity if landing else parity, core, a, 1)]
        return pltpu.make_async_remote_copy(
            src_ref=slot,
            dst_ref=slot,
            send_sem=wz_send.at[i, a],
            recv_sem=wz_recv.at[i, a],
            device_id=device(dz=(3, 1)[a]),
            device_id_type=MESH,
        )

    def weight_over(i, n, landing=False):
        half = parity if n == 0 else 1 - parity
        slot = weights.at[(1 - xl,) + weight_slot(i, half, 1 - core if landing else core, 0, 2)]
        return pltpu.make_async_remote_copy(
            src_ref=slot,
            dst_ref=slot,
            send_sem=wo_send.at[i, n],
            recv_sem=wo_recv.at[i, n],
            device_id=device(dcore=1),
            device_id_type=MESH,
        )

    def weight_start(i):
        for a in range(2):
            weight_hop(i, a).start()

    def weight_pass(i):
        for a in range(2):
            weight_hop(i, a, True).wait_recv()
            weight_along(i, a).start()
        weight_over(i, 0).start()

    def weight_rest(i):
        for a in range(2):
            weight_along(i, a, True).wait_recv()
        weight_over(i, 1).start()

    def weight_ready(i):
        for n in range(2):
            weight_over(i, n, True).wait_recv()

    t_before, t_after, t_far = lax.rem(y + 3, 4), lax.rem(y + 1, 4), lax.rem(y + 2, 4)

    def token_copy(n, landing=False):
        place = (t_before, t_after, t_before, t_after, t_far, t_far)[n] if landing else (y, y, y, y, t_before, t_after)[n]
        h = (0, 1, 1, 0, 0, 1)[n]
        slot = tokens.at[place, pl.ds(h * (rows // 2), rows // 2)]
        return pltpu.make_async_remote_copy(
            src_ref=slot,
            dst_ref=slot,
            send_sem=t_send.at[n],
            recv_sem=t_recv.at[n],
            device_id=device(dy=(1, 3, 1, 3, 1, 3)[n]),
            device_id_type=MESH,
        )

    weight_start(0)
    for h in range(2):
        here = pl.ds(h * (rows // 2), rows // 2)
        normed = layer_norm(x_ref[here].astype(F32)) * (1.0 + scale_ref[...]) + shift_ref[...]
        tokens[y, here] = normed.astype(BF16)
        token_copy(h).start()
    weight_start(1)

    places = [y, t_before, t_after, t_far]

    def out_slot(sp_of, h, c):
        start, count = (256 * sp_of, 256) if h is None else (256 * sp_of + 128 * h, 128)
        columns = pl.ds(pl.multiple_of(out_half * c, 128), out_half)
        return w_out.at[pl.ds(pl.multiple_of(start, 128), count), columns]

    def out_piece(i, place):
        return out_slot(2 * place + xl, None, core)

    def out_mate(i, place):
        return out_slot(2 * place + xl, None, 1 - core)

    def out_half_of(i, place, h):
        return out_slot(2 * place + xl, h, core)

    o_ring = Ring(y, device(dy=3), device(dy=1), device(dcore=1), out_piece, out_half_of, o_send, o_recv)

    def side_copy(n, a, landing=False):
        slot = out_slot(2 * places[n] + (1 - xl if landing else xl), a, core)
        return pltpu.make_async_remote_copy(
            src_ref=slot,
            dst_ref=slot,
            send_sem=side_send.at[n, a],
            recv_sem=side_recv.at[n, a],
            device_id=flip(a, 1),
            device_id_type=MESH,
        )

    def over_copy(n, landing=False):
        slot = out_slot(2 * places[n] + 1 - xl, None, 1 - core if landing else core)
        return pltpu.make_async_remote_copy(
            src_ref=slot,
            dst_ref=slot,
            send_sem=over_send.at[n],
            recv_sem=over_recv.at[n],
            device_id=device(dcore=1),
            device_id_type=MESH,
        )

    def send_sideways(n):
        for a in range(2):
            side_copy(n, a).start()

    def send_over(n):
        for a in range(2):
            side_copy(n, a, True).wait_recv()
        over_copy(n).start()

    scale = HD ** (-0.5) / math.log(2.0)
    q_gain = q_gain_ref[...] * scale
    k_gain = k_gain_ref[...]
    block = 2 * z + core

    def finish_part(part, values):
        if part == 2:
            return values.astype(BF16)
        return rms_scale(values, q_gain if part == 0 else k_gain).astype(BF16)

    def token_rows(j):
        return pl.ds(pl.multiple_of(places[j] * rows, rows), rows)

    def own_copy(j):
        return pltpu.make_async_copy(stage.at[0, j, xh], qkv.at[block, x, :, token_rows(j)], copy_sem.at[j])

    def far_copy(a, j, part, landing=False):
        source = 2 * lax.rem(xh + a, 2) + 1 - xl if landing else x
        slot = qkv.at[block, source, part, token_rows(j)]
        return pltpu.make_async_remote_copy(
            src_ref=slot if landing else stage.at[1, j, lax.rem(xh + a, 2), part],
            dst_ref=slot,
            send_sem=far_send.at[a, j, part],
            recv_sem=far_recv.at[a, j, part],
            device_id=flip(a, 1),
            device_id_type=MESH,
        )

    def near_copy(j, landing=False):
        slot = qkv.at[block, 2 * (1 - xh) + xl if landing else x, :, token_rows(j)]
        return pltpu.make_async_remote_copy(
            src_ref=slot if landing else stage.at[0, j, 1 - xh],
            dst_ref=slot,
            send_sem=near_send.at[j],
            recv_sem=near_recv.at[j],
            device_id=flip(1, 0),
            device_id_type=MESH,
        )

    def heads(b, js, parts):
        seen = jnp.concatenate([tokens[places[j]] for j in js], axis=0)
        for part in parts:
            made = jnp.dot(seen, weights[lax.rem(xl + b, 2), part], preferred_element_type=F32)
            for head in range(2):
                done = finish_part(part, made[:, head * HD : (head + 1) * HD])
                for n, j in enumerate(js):
                    stage[b, j, head, part] = done[n * rows : (n + 1) * rows]
            if b == 1:
                for j in js:
                    for a in range(2):
                        far_copy(a, j, part).start()
        if b == 0:
            for j in js:
                near_copy(j).start()
                own_copy(j).start()

    def far_heads(i, js):
        weight_ready(i)
        heads(1, js, every[i : i + 1])

    weight_pass(0)
    weight_start(2)
    own_weights.wait()
    heads(0, [0], every)
    token_copy(2).start()
    token_copy(3).start()
    own_out.wait()
    send_sideways(0)

    w_text_in.wait()
    row, col = (lax.broadcasted_iota(jnp.int32, (2 * HD, 4 * HD), d) for d in (0, 1))
    chosen = (col == 4 * lax.rem(row, HD) + 2 * xh + lax.div(row, HD)).astype(F32).astype(BF16)

    def choose(n, carry):
        raw = w_text_raw[pl.ds(pl.multiple_of(n * 4 * HD, 4 * HD), 4 * HD)]
        both = jnp.dot(chosen, raw, preferred_element_type=F32).astype(BF16)
        here = pl.ds(pl.multiple_of(n * HD, HD), HD)
        w_text[here, 0:HD] = both[:HD]
        w_text[here, HD:] = both[HD:]
        return carry

    lax.fori_loop(0, width // HD // 3, choose, 0)
    weight_pass(1)
    lax.fori_loop(width // HD // 3, width // HD, choose, 0)
    token_copy(0, True).wait_recv()
    token_copy(4).start()
    token_copy(1, True).wait_recv()
    token_copy(5).start()
    weight_rest(0)
    weight_pass(2)
    token_copy(2, True).wait_recv()
    token_copy(3, True).wait_recv()
    heads(0, [1, 2], every)
    weight_rest(1)
    far_heads(0, [0, 1, 2])
    weight_rest(2)
    far_heads(1, [0, 1, 2])
    far_heads(2, [0, 1, 2])
    token_copy(4, True).wait_recv()
    token_copy(5, True).wait_recv()
    heads(0, [3], every)
    heads(1, [3], every)
    o_ring.start(0, False)

    text_in.wait()
    text_normed = layer_norm(text[...].astype(F32)).astype(BF16)
    text_made = jnp.dot(text_normed, w_text[...], preferred_element_type=F32)
    text_kv[0] = rms_scale(text_made[:, :HD], text_gain_ref[...]).astype(BF16)
    text_kv[1] = text_made[:, HD:].astype(BF16)

    w_taps[...] = jnp.zeros_like(w_taps)
    ch, cv = w_in_ref.shape[3], w_in_ref.shape[4]
    for kt in range(3):
        for kr in range(3):
            for d in range(3):
                for q in range(2):
                    for q_out in range(2):
                        kc = 2 * (d - 1) + q - q_out + 1
                        if 0 <= kc < 3:
                            first = (3 * kt + kr) * HD + (2 * d + q) * ch
                            w_taps[pl.ds(first, ch), pl.ds(cv * q_out, cv)] = w_in_ref[kt, kr, kc]

    sources = [2 * lax.rem(xh + a, 2) + lax.rem(xl + b, 2) for b in range(2) for a in range(2)]

    def kv_piece_of(i, place, c):
        return qkv.at[2 * place + c, sources[i], pl.ds(1, 2)]

    def kv_piece(i, place):
        return kv_piece_of(i, place, core)

    def kv_half(i, place, h):
        return qkv.at[2 * place + core, sources[i], 1 + h]

    def kv_mate(i, place):
        return kv_piece_of(i, place, 1 - core)

    kv_ring = Ring(z, device(dz=3), device(dz=1), device(dcore=1), kv_piece, kv_half, kv_send, kv_recv)

    for j in range(4):
        own_copy(j).wait()
    kv_ring.start(0, True)
    for j in range(4):
        near_copy(j, True).wait_recv()
    kv_ring.start(1, True)
    for a in range(2):
        for j in range(4):
            for part in range(3):
                far_copy(a, j, part, True).wait_recv()
        kv_ring.start(2 + a, True)

    for i in range(3):
        for n in range(2):
            weight_along(i, n).wait_send()
            weight_over(i, n).wait_send()
    w_mid = weights.at[0, :, pl.ds(0, w_mid_ref.shape[1])]
    w_mid_in = pltpu.make_async_copy(w_mid_ref, w_mid, local_sem.at[4])
    w_mid_in.start()

    q_tile = 2 * keys_here

    def attend(first, keys, values, tile):
        here = pl.ds(tile * q_tile if isinstance(tile, int) else pl.multiple_of(tile * q_tile, q_tile), q_tile)
        one = 2 * (1 - xh) + lax.rem(xl + tile, 2)
        two = 2 * xh + lax.rem(xl + 1 - tile, 2)
        queries = jnp.concatenate([qkv[block, one, 0], qkv[block, two, 0]], axis=0)
        scores = lax.dot_general(queries, keys, (((1,), (1,)), ((), ())), preferred_element_type=F32)
        weight = jnp.exp2(scores).astype(BF16)
        added = weight[:, :HD].astype(F32)
        for k in range(1, keys.shape[0] // HD):
            added = added + weight[:, k * HD : (k + 1) * HD].astype(F32)
        product = jnp.dot(weight, values, preferred_element_type=F32)
        if first:
            totals[here] = added
            acc[here] = product
        else:
            totals[here] += added
            acc[here] += product

    for tile in range(2):
        attend(True, text_kv[0], text_kv[1], tile)

    def chunk_pair(place, other, pair):
        b = 2 * lax.rem(z + place, 4) + lax.rem(core + other, 2)
        first = 2 * xh + lax.rem(xl + pair, 2)
        second = 2 * (1 - xh) + lax.rem(xl + pair, 2)
        keys = jnp.concatenate([qkv[b, first, 1], qkv[b, second, 1]], axis=0)
        values = jnp.concatenate([qkv[b, first, 2], qkv[b, second, 2]], axis=0)
        return keys, values

    def mates(i, j):
        return lambda: kv_ring.landed(i, j, kv_mate)

    def out_along():
        o_ring.forward(0, True)
        send_sideways(1)
        send_sideways(2)

    def out_opposite():
        o_ring.opposite(0, True)
        send_sideways(3)

    def step(t, carry):
        def at(n, work):
            @pl.when(t == n)
            def _():
                work()

        at(1, out_along)
        at(2, lambda: send_over(0))
        at(5, out_opposite)
        at(8, lambda: send_over(1))
        at(9, lambda: send_over(2))
        at(11, lambda: send_over(3))
        at(2, lambda: kv_ring.forward(0, True))
        at(2, mates(0, 2))
        at(2, mates(1, 2))
        at(3, mates(2, 2))
        at(3, mates(3, 2))
        at(4, lambda: kv_ring.forward(1, True))
        at(6, mates(0, 4))
        at(6, mates(1, 4))
        at(6, lambda: kv_ring.forward(2, True))
        at(7, mates(0, 6))
        at(7, mates(1, 6))
        at(8, lambda: kv_ring.forward(3, True))
        at(9, lambda: kv_ring.opposite(0, True))
        at(10, mates(2, 4))
        at(10, mates(3, 4))
        at(10, lambda: kv_ring.opposite(1, True))
        at(11, mates(2, 6))
        at(11, mates(3, 6))
        at(11, lambda: kv_ring.opposite(2, True))
        own = t < 4
        place = jnp.where(own, 0, jnp.where(lax.rem(t, 2) == 0, 3, 1))
        other = jnp.where(own, lax.div(t, 2), lax.div(lax.rem(t, 4), 2))
        pair = jnp.where(own, lax.rem(t, 2), lax.div(t - 4, 4))
        keys, values = chunk_pair(place, other, pair)
        for tile in range(2):
            attend(False, keys, values, tile)
        return carry

    lax.fori_loop(0, 12, step, 0)

    def last_step(tile, pair, carry):
        if tile == 0:

            @pl.when(pair == 0)
            def _():
                mates(0, 7)()
                mates(1, 7)()
                kv_ring.opposite(3, True)

            @pl.when(pair == 1)
            def _():
                mates(2, 7)()
                mates(3, 7)()

        for other in range(2):
            keys, values = chunk_pair(2, other, pair)
            attend(False, keys, values, tile)
        return carry

    head = 2 * sp + xh

    def attended_copy(n, landing=False):
        a, b, dy = plane[n]
        at_head = head
        if landing:
            from_sp = 2 * lax.rem(y + 4 - dy, 4) + lax.rem(xl + b, 2)
            at_head = 2 * from_sp + lax.rem(xh + a, 2)
        slot = att.at[:, pl.ds(pl.multiple_of(at_head * HD, HD), HD)]
        made = slot if landing else att_out.at[((1, 0), (0, 1), (1, 1), (0, 0)).index((a, b)), lax.rem(y + dy, 4)]
        return pltpu.make_async_remote_copy(
            src_ref=made,
            dst_ref=slot,
            send_sem=at_send.at[n],
            recv_sem=at_recv.at[n],
            device_id=on_plane(a, b, dy),
            device_id_type=MESH,
        )

    for tile in range(2):
        lax.fori_loop(0, 2, functools.partial(last_step, tile), 0)
        for r in (2 * tile, 2 * tile + 1):
            here = pl.ds(r * keys_here, keys_here)
            total = jnp.sum(totals[here], axis=-1, keepdims=True)
            att_out[r] = (acc[here] / total).astype(BF16).reshape(4, rows, HD)
            for n in range(4 * r, min(4 * r + 4, len(plane))):
                attended_copy(n).start()
    att[:, pl.ds(pl.multiple_of(head * HD, HD), HD)] = att_out[3, y]

    for j in (4, 6, 7):
        o_ring.landed(0, j, out_mate)
    for n in range(4):
        over_copy(n, True).wait_recv()

    def head_of(n):
        a, b, dy = (plane + [(0, 0, 0)])[n]
        return 2 * (2 * lax.rem(y + 4 - dy, 4) + lax.rem(xl + b, 2)) + lax.rem(xh + a, 2)

    def head_columns(n):
        return pl.ds(pl.multiple_of(head_of(n) * HD, HD), HD)

    def projected(ns, columns):
        seen = jnp.concatenate([att[:, head_columns(n)] for n in ns], axis=1)
        taps = jnp.concatenate([w_out[head_columns(n), columns] for n in ns], axis=0)
        return jnp.dot(seen, taps, preferred_element_type=F32)

    def project(n, carry):
        columns = pl.ds(pl.multiple_of(n * 512, 512), 512)
        sums[:, columns] = projected(range(8), columns)
        return carry

    def project_rest(n, carry):
        columns = pl.ds(pl.multiple_of(n * 512, 512), 512)
        proj = sums[:, columns] + projected(range(8, 16), columns)
        out_ref[:, columns] = (x_ref[:, columns].astype(F32) + gate_ref[:, columns] * proj).astype(BF16)
        return carry

    for n in range(8):
        attended_copy(n, True).wait_recv()
    lax.fori_loop(0, width // 512, project, 0)
    for n in range(8, len(plane)):
        attended_copy(n, True).wait_recv()
    lax.fori_loop(0, width // 512, project_rest, 0)
    final = layer_norm(out_ref[...].astype(F32)).astype(BF16)
    latent = lax.dot_general(final, w_final_ref[...], (((1,), (1,)), ((), ())), preferred_element_type=F32)
    latent = latent.astype(BF16)

    patch = latent.shape[1] // 2
    row, col = (lax.broadcasted_iota(jnp.int32, (rows, rows), d) for d in (0, 1))
    feature, lane = (lax.broadcasted_iota(jnp.int32, (2 * patch, HD), d) for d in (0, 1))
    same = lax.div(row, breadth) == lax.div(col, breadth)
    views = [jnp.zeros((rows, HD), F32)] * 2
    for d in range(3):
        shift = ((col == row + (d - 1)) & same).astype(F32).astype(BF16)
        moved = jnp.dot(shift, latent, preferred_element_type=F32).astype(BF16)
        for p in range(2):
            spread = (feature - p * patch == lane - d * patch) & (lane >= d * patch) & (lane < (d + 1) * patch)
            views[p] += jnp.dot(moved, spread.astype(F32).astype(BF16), preferred_element_type=F32)
    for p in range(2):
        for f in range(2):
            lat[f, pl.ds(p * breadth, breadth)] = views[p][f * breadth : (f + 1) * breadth].astype(BF16)

    def halo_copy(n):
        dg, ds = ways[n]
        return pltpu.make_async_remote_copy(
            src_ref=lat,
            dst_ref=window.at[pl.ds(4 - 2 * dg, 2), pl.ds(2 * breadth * (1 - ds), 2 * breadth)],
            send_sem=halo_send.at[n],
            recv_sem=halo_recv.at[n],
            device_id=(grp + dg, sp + ds),
            device_id_type=MESH,
        )

    for n, (dg, ds) in enumerate(ways):

        @pl.when(inside(dg, ds))
        def _():
            halo_copy(n).start()

    window[pl.ds(4, 2), pl.ds(2 * breadth, 2 * breadth)] = lat[...]

    first_frame = 2 * grp
    starts = []
    for f in range(4):
        clip = clip_ref[jnp.maximum(first_frame - 2 + f, 0)]
        start = 0
        for j in range(clip_ref.shape[0]):
            start = start + jnp.where(clip_ref[j] < clip, 1, 0)
        starts.append(start)

    for n, (dg, ds) in enumerate(ways):

        @pl.when(inside(-dg, -ds))
        def _():
            halo_copy(n).wait_recv()

    def frame_at(f, kt, lowest, size):
        index = jnp.maximum(first_frame - 2 + f - kt, starts[f]) - (first_frame - lowest)
        return jnp.clip(index, 0, size - 1)

    tile = lax.broadcasted_iota(jnp.int32, (4 * breadth, 1), 0)
    outside = ((tile < breadth) & (sp == 0)) | ((tile >= 3 * breadth) & (sp == tiles - 1))
    row, col = (lax.broadcasted_iota(jnp.int32, (4 * breadth, 4 * breadth), d) for d in (0, 1))
    same = lax.div(row, breadth) == lax.div(col, breadth)
    left = ((col == row - 1) & same).astype(F32).astype(BF16)
    right = ((col == row + 1) & same).astype(F32).astype(BF16)
    for f in range(4):
        seen = []
        for kt in range(3):
            index = frame_at(f, kt, 4, 6)
            seen += [window[index, pl.ds(kr * breadth, 4 * breadth)] for kr in range(3)]
        total = jnp.dot(jnp.concatenate(seen, axis=1), w_taps[...], preferred_element_type=F32)
        if f >= 2:
            direct[f - 2] = total[breadth : 3 * breadth]
        act = jnp.where(outside, 0.0, total / (1.0 + jnp.exp(-total))).astype(BF16)
        even, odd = act[:, :cv], act[:, cv:]
        planes[0, f] = jnp.dot(left, odd, preferred_element_type=F32).astype(BF16)
        planes[1, f] = even
        planes[2, f] = odd
        planes[3, f] = jnp.dot(right, even, preferred_element_type=F32).astype(BF16)

    w_mid_in.wait()
    mixed = jnp.zeros((8 * breadth, cv), F32)
    for kt in range(3):
        index = [frame_at(2 + f, kt, 2, 4) for f in range(2)]
        for kr in range(3):
            here = pl.ds(kr * breadth, 2 * breadth)
            seen = [
                jnp.concatenate([planes[q + kc, index[f], here] for kc in range(3)], axis=1)
                for f in range(2)
                for q in range(2)
            ]
            taps = weights[0, kt, pl.ds(3 * cv * kr, 3 * cv)]
            mixed = mixed + jnp.dot(jnp.concatenate(seen, axis=0), taps, preferred_element_type=F32)

    row, col = (lax.broadcasted_iota(jnp.int32, (2 * breadth, 2 * breadth), d) for d in (0, 1))
    woven = (col == lax.div(row, 2) + breadth * lax.rem(row, 2)).astype(F32).astype(BF16)
    for f in range(2):
        for r in range(2):
            pair = []
            for q in range(2):
                start = (2 * f + q) * 2 * breadth + r * breadth
                added = mixed[start : start + breadth] + direct[f, r * breadth : (r + 1) * breadth, q * cv : (q + 1) * cv]
                pair.append(added.astype(BF16))
            dec_ref[f, r] = jnp.dot(woven, jnp.concatenate(pair, axis=0), preferred_element_type=F32).astype(BF16)

    for i in range(3):
        for a in range(2):
            weight_hop(i, a).wait_send()
    for n in range(6):
        token_copy(n).wait_send()
    o_ring.finish(0, (0, 1, 3, 4, 5, 6, 7))
    for j in range(4):
        near_copy(j).wait_send()
        over_copy(j).wait_send()
        for a in range(2):
            side_copy(j, a).wait_send()
            for part in range(3):
                far_copy(a, j, part).wait_send()
        kv_ring.finish(j, range(8))
    for n in range(len(plane)):
        attended_copy(n).wait_send()
    for n, (dg, ds) in enumerate(ways):

        @pl.when(inside(dg, ds))
        def _():
            halo_copy(n).wait_send()


def settle_kernel(block_ref, decoded_ref, block_out_ref, decoded_out_ref):
    block_out_ref[...] = block_ref[...]
    decoded_out_ref[...] = decoded_ref[...]


def per_device(
    image_tokens,
    text_tokens,
    mod_shift,
    mod_scale,
    mod_gate,
    w_qkv,
    w_text_kv,
    q_gain,
    k_gain,
    text_gain,
    w_out,
    w_final,
    w_conv_in,
    w_conv_mid,
    clip_ids,
):
    slab, patch_rows, breadth, width = image_tokens.shape
    rows = slab * patch_rows * breadth
    inner_here = w_qkv.shape[2]
    inner = w_out.shape[0] * lax.axis_size("sp")
    cv = w_conv_in.shape[-1]
    text_count = text_tokens.shape[0]
    w_text = jnp.transpose(w_text_kv.reshape(width, 2, 2, HD), (0, 2, 1, 3)).reshape(4 * width, HD)

    vmem = pl.BlockSpec(memory_space=pltpu.VMEM)
    anywhere = pl.BlockSpec(memory_space=pl.ANY)
    dma = pltpu.SemaphoreType.DMA
    block_flat, decoded = pl.pallas_call(
        whole_kernel,
        out_shape=(
            jax.ShapeDtypeStruct((rows, width), BF16),
            jax.ShapeDtypeStruct((slab, 2 * patch_rows, 2 * breadth, cv), BF16),
        ),
        in_specs=[vmem] * 4
        + [anywhere] * 3
        + [vmem] * 3
        + [anywhere, vmem, vmem, anywhere, pl.BlockSpec(memory_space=pltpu.SMEM)],
        out_specs=(vmem, vmem),
        scratch_shapes=[
            pltpu.VMEM((4, rows, width), BF16),
            pltpu.VMEM((2, 3, width, inner_here), BF16),
            pltpu.VMEM((8, 4, 3, 4 * rows, HD), BF16),
            pltpu.VMEM((2, 4, 2, 3, rows, HD), BF16),
            pltpu.VMEM((16 * rows, HD), F32),
            pltpu.VMEM((16 * rows, HD), F32),
            pltpu.VMEM((inner, width), BF16),
            pltpu.VMEM((4, 4, rows, HD), BF16),
            pltpu.VMEM((rows, inner), BF16),
            pltpu.VMEM((rows, width), F32),
            pltpu.VMEM((text_count, width), BF16),
            pltpu.VMEM((4 * width, HD), BF16),
            pltpu.VMEM((width, 2 * HD), BF16),
            pltpu.VMEM((2, text_count, HD), BF16),
            pltpu.VMEM((2, 2 * breadth, HD), BF16),
            pltpu.VMEM((6, 6 * breadth, HD), BF16),
            pltpu.VMEM((9 * HD, 2 * cv), BF16),
            pltpu.VMEM((4, 4, 4 * breadth, cv), BF16),
            pltpu.VMEM((2, 2 * breadth, 2 * cv), F32),
            dma((5,)),
            dma((4,)),
            dma((3, 2)),
            dma((3, 2)),
            dma((3, 2)),
            dma((3, 2)),
            dma((3, 2)),
            dma((3, 2)),
            dma((6,)),
            dma((6,)),
            dma((1, 8)),
            dma((1, 8)),
            dma((4, 2)),
            dma((4, 2)),
            dma((4,)),
            dma((4,)),
            dma((2, 4, 3)),
            dma((2, 4, 3)),
            dma((4,)),
            dma((4,)),
            dma((4, 8)),
            dma((4, 8)),
            dma((15,)),
            dma((15,)),
            dma((8,)),
            dma((8,)),
        ],
        compiler_params=pltpu.CompilerParams(
            collective_id=0, has_side_effects=True, vmem_limit_bytes=60 * 1024 * 1024
        ),
    )(
        image_tokens.reshape(rows, width),
        mod_shift.reshape(1, width),
        mod_scale.reshape(1, width),
        mod_gate.reshape(1, width),
        jnp.transpose(w_qkv, (1, 0, 2)),
        text_tokens,
        w_text,
        q_gain.reshape(1, HD),
        k_gain.reshape(1, HD),
        text_gain.reshape(1, HD),
        w_out,
        jnp.transpose(w_final),
        w_conv_in,
        w_conv_mid.reshape(3, 9 * cv, cv),
        clip_ids,
    )
    block_flat, decoded = pl.pallas_call(
        settle_kernel,
        out_shape=tuple(jax.ShapeDtypeStruct(made.shape, made.dtype) for made in (block_flat, decoded)),
        in_specs=[vmem] * 2,
        out_specs=(vmem, vmem),
    )(block_flat, decoded)
    return (block_flat.reshape(slab, patch_rows, breadth, width), decoded)


def solution(mesh):
    return jax.shard_map(
        per_device,
        mesh=mesh,
        in_specs=(
            P("grp", "sp", None, None),
            P(),
            P(),
            P(),
            P(),
            P(None, None, "sp"),
            P(None, None, "sp"),
            P(),
            P(),
            P(),
            P("sp", None),
            P(),
            P(),
            P(),
            P(),
        ),
        out_specs=(P("grp", "sp", None, None), P("grp", "sp", None, None)),
        check_vma=False,
    )
```

```python
import functools
import math

import jax
import jax.numpy as jnp
from jax import lax
from jax.experimental import pallas as pl
from jax.experimental.pallas import tpu as pltpu
from jax.sharding import PartitionSpec as P

HD = 128
EPS = 1e-06
MESH = pl.DeviceIdType.MESH
F32 = jnp.float32
BF16 = jnp.bfloat16


def layer_norm(values):
    middle = jnp.mean(values, axis=-1, keepdims=True)
    centered = values - middle
    spread = jnp.mean(centered * centered, axis=-1, keepdims=True)
    return centered * lax.rsqrt(spread + EPS)


def rms_scale(values, gain):
    return values * lax.rsqrt(jnp.mean(values * values, axis=-1, keepdims=True) + EPS) * gain


class Ring:
    def __init__(self, at, before, after, mate, piece, half, send, recv):
        self.at = at
        self.before, self.after, self.mate = before, after, mate
        self.piece, self.half = piece, half
        self.send, self.recv = send, recv

    def copy(self, i, slot, j, device):
        return pltpu.make_async_remote_copy(
            src_ref=slot,
            dst_ref=slot,
            send_sem=self.send.at[i, j],
            recv_sem=self.recv.at[i, j],
            device_id=device,
            device_id_type=MESH,
        )

    def place(self, step):
        return lax.rem(self.at + step, 4)

    def out(self, i, j):
        if j in (0, 1, 2):
            return self.copy(i, self.piece(i, self.at), j, (self.after, self.before, self.mate)[j])
        if j == 3:
            return self.copy(i, self.half(i, self.place(3), 0), j, self.after)
        if j == 5:
            return self.copy(i, self.half(i, self.place(1), 1), j, self.before)
        return self.copy(i, self.piece(i, self.place({4: 3, 6: 1, 7: 2}[j])), j, self.mate)

    def start(self, i, mate):
        for j in (0, 1, 2) if mate else (0, 1):
            self.out(i, j).start()

    def landed(self, i, j, mate_piece=None):
        slot = {
            0: lambda: self.piece(i, self.place(3)),
            1: lambda: self.piece(i, self.place(1)),
            3: lambda: self.half(i, self.place(2), 0),
            5: lambda: self.half(i, self.place(2), 1),
        }
        if j in slot:
            where = slot[j]()
        else:
            where = mate_piece(i, self.place({2: 0, 4: 3, 6: 1, 7: 2}[j]))
        self.copy(i, where, j, self.after).wait_recv()

    def forward(self, i, mate):
        self.landed(i, 0)
        self.out(i, 3).start()
        self.landed(i, 1)
        self.out(i, 5).start()
        if mate:
            self.out(i, 4).start()
            self.out(i, 6).start()

    def opposite(self, i, mate):
        self.landed(i, 3)
        self.landed(i, 5)
        if mate:
            self.out(i, 7).start()

    def finish(self, i, js):
        for j in js:
            self.out(i, j).wait_send()


def whole_kernel(
    x_ref,
    shift_ref,
    scale_ref,
    gate_ref,
    w_qkv_ref,
    text_ref,
    w_text_ref,
    q_gain_ref,
    k_gain_ref,
    text_gain_ref,
    w_out_ref,
    w_final_ref,
    w_in_ref,
    w_mid_ref,
    clip_ref,
    out_ref,
    dec_ref,
    tokens,
    weights,
    qkv,
    stage,
    acc,
    totals,
    w_out,
    att_out,
    att,
    sums,
    text,
    w_text_raw,
    w_text,
    text_kv,
    lat,
    window,
    w_taps,
    planes,
    direct,
    local_sem,
    copy_sem,
    wx_send,
    wx_recv,
    wz_send,
    wz_recv,
    wo_send,
    wo_recv,
    t_send,
    t_recv,
    o_send,
    o_recv,
    side_send,
    side_recv,
    over_send,
    over_recv,
    far_send,
    far_recv,
    near_send,
    near_recv,
    kv_send,
    kv_recv,
    at_send,
    at_recv,
    halo_send,
    halo_recv,
):
    grp, sp = lax.axis_index("grp"), lax.axis_index("sp")
    z, xh, core = lax.div(grp, 4), lax.rem(lax.div(grp, 2), 2), lax.rem(grp, 2)
    y, xl = lax.div(sp, 2), lax.rem(sp, 2)
    x = 2 * xh + xl
    rows, width = x_ref.shape
    keys_here = 4 * rows
    out_half = width // 2

    def device(dz=0, dxh=0, dcore=0, dy=0, dxl=0):
        new_grp = 4 * lax.rem(z + dz, 4) + 2 * lax.rem(xh + dxh, 2) + lax.rem(core + dcore, 2)
        new_sp = 2 * lax.rem(y + dy, 4) + lax.rem(xl + dxl, 2)
        return (new_grp, new_sp)

    def flip(a, b):
        return device(dxh=a, dxl=b)

    own_weights = pltpu.make_async_copy(w_qkv_ref, weights.at[xl], local_sem.at[0])
    own_weights.start()
    text_in = pltpu.make_async_copy(text_ref, text, local_sem.at[1])
    text_in.start()
    w_text_in = pltpu.make_async_copy(w_text_ref, w_text_raw, local_sem.at[2])
    w_text_in.start()
    out_rows = pl.ds(pl.multiple_of(256 * sp, 256), 256)
    own_out = pltpu.make_async_copy(w_out_ref, w_out.at[out_rows], local_sem.at[3])
    own_out.start()

    plane = [(a, b, dy) for a, b in ((1, 0), (0, 1), (1, 1), (0, 0)) for dy in (2, 1, 3, 0) if a or b or dy]

    def on_plane(a, b, dy):
        return device(dxh=a, dxl=b, dy=dy)

    slabs, tiles = lax.axis_size("grp"), lax.axis_size("sp")
    ways = [(dg, ds) for dg in range(3) for ds in (-1, 0, 1) if dg or ds]

    def inside(dg, ds):
        g, s = grp + dg, sp + ds
        return (g >= 0) & (g < slabs) & (s >= 0) & (s < tiles)

    barrier = pltpu.get_barrier_semaphore()
    partners = [device(dz=1), device(dz=3), device(dcore=1)] + [on_plane(*place) for place in plane]
    for partner in partners:
        pl.semaphore_signal(barrier, inc=1, device_id=partner, device_id_type=MESH)
    expected = len(partners)
    for dg in (-2, -1, 0, 1, 2):
        for ds in (-1, 0, 1):
            if dg or ds:
                there = inside(dg, ds)

                @pl.when(there)
                def _():
                    pl.semaphore_signal(barrier, inc=1, device_id=(grp + dg, sp + ds), device_id_type=MESH)

                expected = expected + jnp.where(there, 1, 0)

    breadth = rows // 2
    zero_rows = jnp.zeros((6, 2 * breadth, HD), BF16)

    @pl.when(sp == 0)
    def _():
        window[:, 0 : 2 * breadth] = zero_rows

    @pl.when(sp == tiles - 1)
    def _():
        window[:, 4 * breadth :] = zero_rows

    for first in (0, 1):

        @pl.when(grp == first)
        def _():
            window[0 : 4 - 2 * first] = jnp.zeros((4 - 2 * first, 6 * breadth, HD), BF16)

    for h in range(2):
        here = pl.ds(h * (rows // 2), rows // 2)
        normed = layer_norm(x_ref[here].astype(F32)) * (1.0 + scale_ref[...]) + shift_ref[...]
        tokens[y, here] = normed.astype(BF16)

    pl.semaphore_wait(barrier, expected)

    eighth = width // 8
    every = (1, 2, 0)

    def weight_slot(i, half, c, first, count):
        start = eighth * (4 * half + 2 * c + first)
        return (every[i], pl.ds(pl.multiple_of(start, eighth), eighth * count))

    parity = lax.rem(z, 2)

    def weight_hop(i, a, landing=False):
        here = weight_slot(i, parity, core, a, 1)
        slot = weights.at[(1 - xl if landing else xl,) + here]
        return pltpu.make_async_remote_copy(
            src_ref=slot if landing else w_qkv_ref.at[here],
            dst_ref=slot,
            send_sem=wx_send.at[i, a],
            recv_sem=wx_recv.at[i, a],
            device_id=flip(a, 1),
            device_id_type=MESH,
        )

    def weight_along(i, a, landing=False):
        slot = weights.at[(1 - xl,) + weight_slot(i, 1 - parity if landing else parity, core, a, 1)]
        return pltpu.make_async_remote_copy(
            src_ref=slot,
            dst_ref=slot,
            send_sem=wz_send.at[i, a],
            recv_sem=wz_recv.at[i, a],
            device_id=device(dz=(3, 1)[a]),
            device_id_type=MESH,
        )

    def weight_over(i, n, landing=False):
        half = parity if n == 0 else 1 - parity
        slot = weights.at[(1 - xl,) + weight_slot(i, half, 1 - core if landing else core, 0, 2)]
        return pltpu.make_async_remote_copy(
            src_ref=slot,
            dst_ref=slot,
            send_sem=wo_send.at[i, n],
            recv_sem=wo_recv.at[i, n],
            device_id=device(dcore=1),
            device_id_type=MESH,
        )

    def weight_start(i):
        for a in range(2):
            weight_hop(i, a).start()

    def weight_pass(i):
        for a in range(2):
            weight_hop(i, a, True).wait_recv()
            weight_along(i, a).start()
        weight_over(i, 0).start()

    def weight_rest(i):
        for a in range(2):
            weight_along(i, a, True).wait_recv()
        weight_over(i, 1).start()

    def weight_ready(i):
        for n in range(2):
            weight_over(i, n, True).wait_recv()

    t_before, t_after, t_far = lax.rem(y + 3, 4), lax.rem(y + 1, 4), lax.rem(y + 2, 4)

    def token_copy(n, landing=False):
        place = (t_before, t_after, t_before, t_after, t_far, t_far)[n] if landing else (y, y, y, y, t_before, t_after)[n]
        h = (0, 1, 1, 0, 0, 1)[n]
        slot = tokens.at[place, pl.ds(h * (rows // 2), rows // 2)]
        return pltpu.make_async_remote_copy(
            src_ref=slot,
            dst_ref=slot,
            send_sem=t_send.at[n],
            recv_sem=t_recv.at[n],
            device_id=device(dy=(1, 3, 1, 3, 1, 3)[n]),
            device_id_type=MESH,
        )

    token_copy(0).start()
    token_copy(1).start()
    weight_start(0)
    weight_start(1)

    places = [y, t_before, t_after, t_far]

    def out_slot(sp_of, h, c):
        start, count = (256 * sp_of, 256) if h is None else (256 * sp_of + 128 * h, 128)
        columns = pl.ds(pl.multiple_of(out_half * c, 128), out_half)
        return w_out.at[pl.ds(pl.multiple_of(start, 128), count), columns]

    def out_piece(i, place):
        return out_slot(2 * place + xl, None, core)

    def out_mate(i, place):
        return out_slot(2 * place + xl, None, 1 - core)

    def out_half_of(i, place, h):
        return out_slot(2 * place + xl, h, core)

    o_ring = Ring(y, device(dy=3), device(dy=1), device(dcore=1), out_piece, out_half_of, o_send, o_recv)

    def side_copy(n, a, landing=False):
        slot = out_slot(2 * places[n] + (1 - xl if landing else xl), a, core)
        return pltpu.make_async_remote_copy(
            src_ref=slot,
            dst_ref=slot,
            send_sem=side_send.at[n, a],
            recv_sem=side_recv.at[n, a],
            device_id=flip(a, 1),
            device_id_type=MESH,
        )

    def over_copy(n, landing=False):
        slot = out_slot(2 * places[n] + 1 - xl, None, 1 - core if landing else core)
        return pltpu.make_async_remote_copy(
            src_ref=slot,
            dst_ref=slot,
            send_sem=over_send.at[n],
            recv_sem=over_recv.at[n],
            device_id=device(dcore=1),
            device_id_type=MESH,
        )

    def send_sideways(n):
        for a in range(2):
            side_copy(n, a).start()

    def send_over(n):
        for a in range(2):
            side_copy(n, a, True).wait_recv()
        over_copy(n).start()

    scale = HD ** (-0.5) / math.log(2.0)
    q_gain = q_gain_ref[...] * scale
    k_gain = k_gain_ref[...]
    block = 2 * z + core

    def finish_part(part, values):
        if part == 2:
            return values.astype(BF16)
        return rms_scale(values, q_gain if part == 0 else k_gain).astype(BF16)

    def token_rows(j):
        return pl.ds(pl.multiple_of(places[j] * rows, rows), rows)

    def own_copy(j):
        return pltpu.make_async_copy(stage.at[0, j, xh], qkv.at[block, x, :, token_rows(j)], copy_sem.at[j])

    def far_copy(a, j, part, landing=False):
        source = 2 * lax.rem(xh + a, 2) + 1 - xl if landing else x
        slot = qkv.at[block, source, part, token_rows(j)]
        return pltpu.make_async_remote_copy(
            src_ref=slot if landing else stage.at[1, j, lax.rem(xh + a, 2), part],
            dst_ref=slot,
            send_sem=far_send.at[a, j, part],
            recv_sem=far_recv.at[a, j, part],
            device_id=flip(a, 1),
            device_id_type=MESH,
        )

    def near_copy(j, landing=False):
        slot = qkv.at[block, 2 * (1 - xh) + xl if landing else x, :, token_rows(j)]
        return pltpu.make_async_remote_copy(
            src_ref=slot if landing else stage.at[0, j, 1 - xh],
            dst_ref=slot,
            send_sem=near_send.at[j],
            recv_sem=near_recv.at[j],
            device_id=flip(1, 0),
            device_id_type=MESH,
        )

    def heads(b, js, parts):
        seen = jnp.concatenate([tokens[places[j]] for j in js], axis=0)
        for part in parts:
            made = jnp.dot(seen, weights[lax.rem(xl + b, 2), part], preferred_element_type=F32)
            for head in range(2):
                done = finish_part(part, made[:, head * HD : (head + 1) * HD])
                for n, j in enumerate(js):
                    stage[b, j, head, part] = done[n * rows : (n + 1) * rows]
            if b == 1:
                for j in js:
                    for a in range(2):
                        far_copy(a, j, part).start()
        if b == 0:
            for j in js:
                near_copy(j).start()
                own_copy(j).start()

    def far_heads(i, js):
        weight_ready(i)
        heads(1, js, every[i : i + 1])

    weight_pass(0)
    weight_start(2)
    own_weights.wait()
    heads(0, [0], every)
    token_copy(2).start()
    token_copy(3).start()
    own_out.wait()
    send_sideways(0)

    w_text_in.wait()
    row, col = (lax.broadcasted_iota(jnp.int32, (2 * HD, 4 * HD), d) for d in (0, 1))
    chosen = (col == 4 * lax.rem(row, HD) + 2 * xh + lax.div(row, HD)).astype(F32).astype(BF16)

    def choose(n, carry):
        raw = w_text_raw[pl.ds(pl.multiple_of(n * 4 * HD, 4 * HD), 4 * HD)]
        both = jnp.dot(chosen, raw, preferred_element_type=F32).astype(BF16)
        here = pl.ds(pl.multiple_of(n * HD, HD), HD)
        w_text[here, 0:HD] = both[:HD]
        w_text[here, HD:] = both[HD:]
        return carry

    lax.fori_loop(0, width // HD // 3, choose, 0)
    weight_pass(1)
    lax.fori_loop(width // HD // 3, width // HD, choose, 0)
    token_copy(0, True).wait_recv()
    token_copy(4).start()
    token_copy(1, True).wait_recv()
    token_copy(5).start()
    weight_rest(0)
    weight_pass(2)
    token_copy(2, True).wait_recv()
    token_copy(3, True).wait_recv()
    heads(0, [1, 2], every)
    weight_rest(1)
    far_heads(0, [0, 1, 2])
    weight_rest(2)
    far_heads(1, [0, 1, 2])
    far_heads(2, [0, 1, 2])
    token_copy(4, True).wait_recv()
    token_copy(5, True).wait_recv()
    heads(0, [3], every)
    heads(1, [3], every)
    o_ring.start(0, False)

    text_in.wait()
    text_normed = layer_norm(text[...].astype(F32)).astype(BF16)
    text_made = jnp.dot(text_normed, w_text[...], preferred_element_type=F32)
    text_kv[0] = rms_scale(text_made[:, :HD], text_gain_ref[...]).astype(BF16)
    text_kv[1] = text_made[:, HD:].astype(BF16)

    w_taps[...] = jnp.zeros_like(w_taps)
    ch, cv = w_in_ref.shape[3], w_in_ref.shape[4]
    for kt in range(3):
        for kr in range(3):
            for d in range(3):
                for q in range(2):
                    for q_out in range(2):
                        kc = 2 * (d - 1) + q - q_out + 1
                        if 0 <= kc < 3:
                            first = (3 * kt + kr) * HD + (2 * d + q) * ch
                            w_taps[pl.ds(first, ch), pl.ds(cv * q_out, cv)] = w_in_ref[kt, kr, kc]

    sources = [2 * lax.rem(xh + a, 2) + lax.rem(xl + b, 2) for b in range(2) for a in range(2)]

    def kv_piece_of(i, place, c):
        return qkv.at[2 * place + c, sources[i], pl.ds(1, 2)]

    def kv_piece(i, place):
        return kv_piece_of(i, place, core)

    def kv_half(i, place, h):
        return qkv.at[2 * place + core, sources[i], 1 + h]

    def kv_mate(i, place):
        return kv_piece_of(i, place, 1 - core)

    kv_ring = Ring(z, device(dz=3), device(dz=1), device(dcore=1), kv_piece, kv_half, kv_send, kv_recv)

    for j in range(4):
        own_copy(j).wait()
    kv_ring.start(0, True)
    for j in range(4):
        near_copy(j, True).wait_recv()
    kv_ring.start(1, True)
    for a in range(2):
        for j in range(4):
            for part in range(3):
                far_copy(a, j, part, True).wait_recv()
        kv_ring.start(2 + a, True)

    for i in range(3):
        for n in range(2):
            weight_along(i, n).wait_send()
            weight_over(i, n).wait_send()
    w_mid = weights.at[0, :, pl.ds(0, w_mid_ref.shape[1])]
    w_mid_in = pltpu.make_async_copy(w_mid_ref, w_mid, local_sem.at[4])
    w_mid_in.start()

    q_tile = 2 * keys_here

    def attend(first, keys, values, tile):
        here = pl.ds(tile * q_tile if isinstance(tile, int) else pl.multiple_of(tile * q_tile, q_tile), q_tile)
        one = 2 * (1 - xh) + lax.rem(xl + tile, 2)
        two = 2 * xh + lax.rem(xl + 1 - tile, 2)
        queries = jnp.concatenate([qkv[block, one, 0], qkv[block, two, 0]], axis=0)
        scores = lax.dot_general(queries, keys, (((1,), (1,)), ((), ())), preferred_element_type=F32)
        weight = jnp.exp2(scores).astype(BF16)
        added = weight[:, :HD].astype(F32)
        for k in range(1, keys.shape[0] // HD):
            added = added + weight[:, k * HD : (k + 1) * HD].astype(F32)
        product = jnp.dot(weight, values, preferred_element_type=F32)
        if first:
            totals[here] = added
            acc[here] = product
        else:
            totals[here] += added
            acc[here] += product

    for tile in range(2):
        attend(True, text_kv[0], text_kv[1], tile)

    def chunk_pair(place, other, pair):
        b = 2 * lax.rem(z + place, 4) + lax.rem(core + other, 2)
        first = 2 * xh + lax.rem(xl + pair, 2)
        second = 2 * (1 - xh) + lax.rem(xl + pair, 2)
        keys = jnp.concatenate([qkv[b, first, 1], qkv[b, second, 1]], axis=0)
        values = jnp.concatenate([qkv[b, first, 2], qkv[b, second, 2]], axis=0)
        return keys, values

    def mates(i, j):
        return lambda: kv_ring.landed(i, j, kv_mate)

    def out_along():
        o_ring.forward(0, True)
        send_sideways(1)
        send_sideways(2)

    def out_opposite():
        o_ring.opposite(0, True)
        send_sideways(3)

    def step(t, carry):
        def at(n, work):
            @pl.when(t == n)
            def _():
                work()

        at(1, out_along)
        at(2, lambda: send_over(0))
        at(5, out_opposite)
        at(8, lambda: send_over(1))
        at(9, lambda: send_over(2))
        at(11, lambda: send_over(3))
        at(2, lambda: kv_ring.forward(0, True))
        at(2, mates(0, 2))
        at(2, mates(1, 2))
        at(3, mates(2, 2))
        at(3, mates(3, 2))
        at(4, lambda: kv_ring.forward(1, True))
        at(6, mates(0, 4))
        at(6, mates(1, 4))
        at(6, lambda: kv_ring.forward(2, True))
        at(7, mates(0, 6))
        at(7, mates(1, 6))
        at(8, lambda: kv_ring.forward(3, True))
        at(9, lambda: kv_ring.opposite(0, True))
        at(10, mates(2, 4))
        at(10, mates(3, 4))
        at(10, lambda: kv_ring.opposite(1, True))
        at(11, mates(2, 6))
        at(11, mates(3, 6))
        at(11, lambda: kv_ring.opposite(2, True))
        own = t < 4
        place = jnp.where(own, 0, jnp.where(lax.rem(t, 2) == 0, 3, 1))
        other = jnp.where(own, lax.div(t, 2), lax.div(lax.rem(t, 4), 2))
        pair = jnp.where(own, lax.rem(t, 2), lax.div(t - 4, 4))
        keys, values = chunk_pair(place, other, pair)
        for tile in range(2):
            attend(False, keys, values, tile)
        return carry

    lax.fori_loop(0, 12, step, 0)

    def last_step(tile, pair, carry):
        if tile == 0:

            @pl.when(pair == 0)
            def _():
                mates(0, 7)()
                mates(1, 7)()
                kv_ring.opposite(3, True)

            @pl.when(pair == 1)
            def _():
                mates(2, 7)()
                mates(3, 7)()

        for other in range(2):
            keys, values = chunk_pair(2, other, pair)
            attend(False, keys, values, tile)
        return carry

    head = 2 * sp + xh

    def attended_copy(n, landing=False):
        a, b, dy = plane[n]
        at_head = head
        if landing:
            from_sp = 2 * lax.rem(y + 4 - dy, 4) + lax.rem(xl + b, 2)
            at_head = 2 * from_sp + lax.rem(xh + a, 2)
        slot = att.at[:, pl.ds(pl.multiple_of(at_head * HD, HD), HD)]
        made = slot if landing else att_out.at[((1, 0), (0, 1), (1, 1), (0, 0)).index((a, b)), lax.rem(y + dy, 4)]
        return pltpu.make_async_remote_copy(
            src_ref=made,
            dst_ref=slot,
            send_sem=at_send.at[n],
            recv_sem=at_recv.at[n],
            device_id=on_plane(a, b, dy),
            device_id_type=MESH,
        )

    for tile in range(2):
        lax.fori_loop(0, 2, functools.partial(last_step, tile), 0)
        for r in (2 * tile, 2 * tile + 1):
            here = pl.ds(r * keys_here, keys_here)
            total = jnp.sum(totals[here], axis=-1, keepdims=True)
            att_out[r] = (acc[here] / total).astype(BF16).reshape(4, rows, HD)
            for n in range(4 * r, min(4 * r + 4, len(plane))):
                attended_copy(n).start()
    att[:, pl.ds(pl.multiple_of(head * HD, HD), HD)] = att_out[3, y]

    for j in (4, 6, 7):
        o_ring.landed(0, j, out_mate)
    for n in range(4):
        over_copy(n, True).wait_recv()

    def head_of(n):
        a, b, dy = (plane + [(0, 0, 0)])[n]
        return 2 * (2 * lax.rem(y + 4 - dy, 4) + lax.rem(xl + b, 2)) + lax.rem(xh + a, 2)

    def head_columns(n):
        return pl.ds(pl.multiple_of(head_of(n) * HD, HD), HD)

    def projected(ns, columns):
        seen = jnp.concatenate([att[:, head_columns(n)] for n in ns], axis=1)
        taps = jnp.concatenate([w_out[head_columns(n), columns] for n in ns], axis=0)
        return jnp.dot(seen, taps, preferred_element_type=F32)

    def project(n, carry):
        columns = pl.ds(pl.multiple_of(n * 512, 512), 512)
        sums[:, columns] = projected(range(8), columns)
        return carry

    def project_rest(n, carry):
        columns = pl.ds(pl.multiple_of(n * 512, 512), 512)
        proj = sums[:, columns] + projected(range(8, 16), columns)
        out_ref[:, columns] = (x_ref[:, columns].astype(F32) + gate_ref[:, columns] * proj).astype(BF16)
        return carry

    for n in range(8):
        attended_copy(n, True).wait_recv()
    lax.fori_loop(0, width // 512, project, 0)
    for n in range(8, len(plane)):
        attended_copy(n, True).wait_recv()
    lax.fori_loop(0, width // 512, project_rest, 0)
    final = layer_norm(out_ref[...].astype(F32)).astype(BF16)
    latent = lax.dot_general(final, w_final_ref[...], (((1,), (1,)), ((), ())), preferred_element_type=F32)
    latent = latent.astype(BF16)

    patch = latent.shape[1] // 2
    row, col = (lax.broadcasted_iota(jnp.int32, (rows, rows), d) for d in (0, 1))
    feature, lane = (lax.broadcasted_iota(jnp.int32, (2 * patch, HD), d) for d in (0, 1))
    same = lax.div(row, breadth) == lax.div(col, breadth)
    views = [jnp.zeros((rows, HD), F32)] * 2
    for d in range(3):
        shift = ((col == row + (d - 1)) & same).astype(F32).astype(BF16)
        moved = jnp.dot(shift, latent, preferred_element_type=F32).astype(BF16)
        for p in range(2):
            spread = (feature - p * patch == lane - d * patch) & (lane >= d * patch) & (lane < (d + 1) * patch)
            views[p] += jnp.dot(moved, spread.astype(F32).astype(BF16), preferred_element_type=F32)
    for p in range(2):
        for f in range(2):
            lat[f, pl.ds(p * breadth, breadth)] = views[p][f * breadth : (f + 1) * breadth].astype(BF16)

    def halo_copy(n):
        dg, ds = ways[n]
        return pltpu.make_async_remote_copy(
            src_ref=lat,
            dst_ref=window.at[pl.ds(4 - 2 * dg, 2), pl.ds(2 * breadth * (1 - ds), 2 * breadth)],
            send_sem=halo_send.at[n],
            recv_sem=halo_recv.at[n],
            device_id=(grp + dg, sp + ds),
            device_id_type=MESH,
        )

    for n, (dg, ds) in enumerate(ways):

        @pl.when(inside(dg, ds))
        def _():
            halo_copy(n).start()

    window[pl.ds(4, 2), pl.ds(2 * breadth, 2 * breadth)] = lat[...]

    first_frame = 2 * grp
    starts = []
    for f in range(4):
        clip = clip_ref[jnp.maximum(first_frame - 2 + f, 0)]
        start = 0
        for j in range(clip_ref.shape[0]):
            start = start + jnp.where(clip_ref[j] < clip, 1, 0)
        starts.append(start)

    for n, (dg, ds) in enumerate(ways):

        @pl.when(inside(-dg, -ds))
        def _():
            halo_copy(n).wait_recv()

    def frame_at(f, kt, lowest, size):
        index = jnp.maximum(first_frame - 2 + f - kt, starts[f]) - (first_frame - lowest)
        return jnp.clip(index, 0, size - 1)

    tile = lax.broadcasted_iota(jnp.int32, (4 * breadth, 1), 0)
    outside = ((tile < breadth) & (sp == 0)) | ((tile >= 3 * breadth) & (sp == tiles - 1))
    row, col = (lax.broadcasted_iota(jnp.int32, (4 * breadth, 4 * breadth), d) for d in (0, 1))
    same = lax.div(row, breadth) == lax.div(col, breadth)
    left = ((col == row - 1) & same).astype(F32).astype(BF16)
    right = ((col == row + 1) & same).astype(F32).astype(BF16)
    for f in range(4):
        seen = []
        for kt in range(3):
            index = frame_at(f, kt, 4, 6)
            seen += [window[index, pl.ds(kr * breadth, 4 * breadth)] for kr in range(3)]
        total = jnp.dot(jnp.concatenate(seen, axis=1), w_taps[...], preferred_element_type=F32)
        if f >= 2:
            direct[f - 2] = total[breadth : 3 * breadth]
        act = jnp.where(outside, 0.0, total / (1.0 + jnp.exp(-total))).astype(BF16)
        even, odd = act[:, :cv], act[:, cv:]
        planes[0, f] = jnp.dot(left, odd, preferred_element_type=F32).astype(BF16)
        planes[1, f] = even
        planes[2, f] = odd
        planes[3, f] = jnp.dot(right, even, preferred_element_type=F32).astype(BF16)

    w_mid_in.wait()
    mixed = jnp.zeros((8 * breadth, cv), F32)
    for kt in range(3):
        index = [frame_at(2 + f, kt, 2, 4) for f in range(2)]
        for kr in range(3):
            here = pl.ds(kr * breadth, 2 * breadth)
            seen = [
                jnp.concatenate([planes[q + kc, index[f], here] for kc in range(3)], axis=1)
                for f in range(2)
                for q in range(2)
            ]
            taps = weights[0, kt, pl.ds(3 * cv * kr, 3 * cv)]
            mixed = mixed + jnp.dot(jnp.concatenate(seen, axis=0), taps, preferred_element_type=F32)

    row, col = (lax.broadcasted_iota(jnp.int32, (2 * breadth, 2 * breadth), d) for d in (0, 1))
    woven = (col == lax.div(row, 2) + breadth * lax.rem(row, 2)).astype(F32).astype(BF16)
    for f in range(2):
        for r in range(2):
            pair = []
            for q in range(2):
                start = (2 * f + q) * 2 * breadth + r * breadth
                added = mixed[start : start + breadth] + direct[f, r * breadth : (r + 1) * breadth, q * cv : (q + 1) * cv]
                pair.append(added.astype(BF16))
            dec_ref[f, r] = jnp.dot(woven, jnp.concatenate(pair, axis=0), preferred_element_type=F32).astype(BF16)

    for i in range(3):
        for a in range(2):
            weight_hop(i, a).wait_send()
    for n in range(6):
        token_copy(n).wait_send()
    o_ring.finish(0, (0, 1, 3, 4, 5, 6, 7))
    for j in range(4):
        near_copy(j).wait_send()
        over_copy(j).wait_send()
        for a in range(2):
            side_copy(j, a).wait_send()
            for part in range(3):
                far_copy(a, j, part).wait_send()
        kv_ring.finish(j, range(8))
    for n in range(len(plane)):
        attended_copy(n).wait_send()
    for n, (dg, ds) in enumerate(ways):

        @pl.when(inside(dg, ds))
        def _():
            halo_copy(n).wait_send()


def settle_kernel(block_ref, decoded_ref, block_out_ref, decoded_out_ref):
    block_out_ref[...] = block_ref[...]
    decoded_out_ref[...] = decoded_ref[...]


def per_device(
    image_tokens,
    text_tokens,
    mod_shift,
    mod_scale,
    mod_gate,
    w_qkv,
    w_text_kv,
    q_gain,
    k_gain,
    text_gain,
    w_out,
    w_final,
    w_conv_in,
    w_conv_mid,
    clip_ids,
):
    slab, patch_rows, breadth, width = image_tokens.shape
    rows = slab * patch_rows * breadth
    inner_here = w_qkv.shape[2]
    inner = w_out.shape[0] * lax.axis_size("sp")
    cv = w_conv_in.shape[-1]
    text_count = text_tokens.shape[0]
    w_text = jnp.transpose(w_text_kv.reshape(width, 2, 2, HD), (0, 2, 1, 3)).reshape(4 * width, HD)

    vmem = pl.BlockSpec(memory_space=pltpu.VMEM)
    anywhere = pl.BlockSpec(memory_space=pl.ANY)
    dma = pltpu.SemaphoreType.DMA
    block_flat, decoded = pl.pallas_call(
        whole_kernel,
        out_shape=(
            jax.ShapeDtypeStruct((rows, width), BF16),
            jax.ShapeDtypeStruct((slab, 2 * patch_rows, 2 * breadth, cv), BF16),
        ),
        in_specs=[vmem] * 4
        + [anywhere] * 3
        + [vmem] * 3
        + [anywhere, vmem, vmem, anywhere, pl.BlockSpec(memory_space=pltpu.SMEM)],
        out_specs=(vmem, vmem),
        scratch_shapes=[
            pltpu.VMEM((4, rows, width), BF16),
            pltpu.VMEM((2, 3, width, inner_here), BF16),
            pltpu.VMEM((8, 4, 3, 4 * rows, HD), BF16),
            pltpu.VMEM((2, 4, 2, 3, rows, HD), BF16),
            pltpu.VMEM((16 * rows, HD), F32),
            pltpu.VMEM((16 * rows, HD), F32),
            pltpu.VMEM((inner, width), BF16),
            pltpu.VMEM((4, 4, rows, HD), BF16),
            pltpu.VMEM((rows, inner), BF16),
            pltpu.VMEM((rows, width), F32),
            pltpu.VMEM((text_count, width), BF16),
            pltpu.VMEM((4 * width, HD), BF16),
            pltpu.VMEM((width, 2 * HD), BF16),
            pltpu.VMEM((2, text_count, HD), BF16),
            pltpu.VMEM((2, 2 * breadth, HD), BF16),
            pltpu.VMEM((6, 6 * breadth, HD), BF16),
            pltpu.VMEM((9 * HD, 2 * cv), BF16),
            pltpu.VMEM((4, 4, 4 * breadth, cv), BF16),
            pltpu.VMEM((2, 2 * breadth, 2 * cv), F32),
            dma((5,)),
            dma((4,)),
            dma((3, 2)),
            dma((3, 2)),
            dma((3, 2)),
            dma((3, 2)),
            dma((3, 2)),
            dma((3, 2)),
            dma((6,)),
            dma((6,)),
            dma((1, 8)),
            dma((1, 8)),
            dma((4, 2)),
            dma((4, 2)),
            dma((4,)),
            dma((4,)),
            dma((2, 4, 3)),
            dma((2, 4, 3)),
            dma((4,)),
            dma((4,)),
            dma((4, 8)),
            dma((4, 8)),
            dma((15,)),
            dma((15,)),
            dma((8,)),
            dma((8,)),
        ],
        compiler_params=pltpu.CompilerParams(
            collective_id=0, has_side_effects=True, vmem_limit_bytes=60 * 1024 * 1024
        ),
    )(
        image_tokens.reshape(rows, width),
        mod_shift.reshape(1, width),
        mod_scale.reshape(1, width),
        mod_gate.reshape(1, width),
        jnp.transpose(w_qkv, (1, 0, 2)),
        text_tokens,
        w_text,
        q_gain.reshape(1, HD),
        k_gain.reshape(1, HD),
        text_gain.reshape(1, HD),
        w_out,
        jnp.transpose(w_final),
        w_conv_in,
        w_conv_mid.reshape(3, 9 * cv, cv),
        clip_ids,
    )
    block_flat, decoded = pl.pallas_call(
        settle_kernel,
        out_shape=tuple(jax.ShapeDtypeStruct(made.shape, made.dtype) for made in (block_flat, decoded)),
        in_specs=[vmem] * 2,
        out_specs=(vmem, vmem),
    )(block_flat, decoded)
    return (block_flat.reshape(slab, patch_rows, breadth, width), decoded)


def solution(mesh):
    return jax.shard_map(
        per_device,
        mesh=mesh,
        in_specs=(
            P("grp", "sp", None, None),
            P(),
            P(),
            P(),
            P(),
            P(None, None, "sp"),
            P(None, None, "sp"),
            P(),
            P(),
            P(),
            P("sp", None),
            P(),
            P(),
            P(),
            P(),
        ),
        out_specs=(P("grp", "sp", None, None), P("grp", "sp", None, None)),
        check_vma=False,
    )
```
